128 devices in a mesh: ep: 8 (over y, core), dp: 16 (over z, x).
Axes of the slice: x: 4, y: 4, z: 4, core: 2. Of those that a mesh axis runs over, the one named last changes fastest.
Arguments:
- hidden_state: bfloat16 [16384, 2048], P(('dp', 'ep')), may hold values from -6 to 6
- out_grad: bfloat16 [16384, 2048], P(('dp', 'ep')), may hold values from -6 to 6
- norm_gain: bfloat16 [2048], replicated, may hold values from 0.5 to 1.5
- expert_ids: int32 [16384, 8], P(('dp', 'ep')), may hold values from 0 to 127, all different within a row; in each aligned block of 128 rows (0 to 127, 128 to 255, ...) at most 10 rows name the same one
- route_weight: bfloat16 [16384, 8], P(('dp', 'ep')), may hold values from 0.019897461 to 0.3984375
- w_gate: bfloat16 [128, 2048, 512], P(('ep', 'dp')), may hold values from -0.125 to 0.125
- w_up: bfloat16 [128, 2048, 512], P(('ep', 'dp')), may hold values from -0.125 to 0.125
- w_down: bfloat16 [128, 512, 2048], P(('ep', 'dp')), may hold values from -0.25 to 0.25
- queries: bfloat16 [16384, 2048], P('dp', 'ep'), may hold values from -6 to 6
- keys: bfloat16 [16384, 2048], P('dp', 'ep'), may hold values from -6 to 6
- values: bfloat16 [16384, 2048], P('dp', 'ep'), may hold values from -6 to 6
- attn_out: bfloat16 [16384, 2048], P('dp', 'ep'), may hold values from -4 to 4
- out_weight: bfloat16 [2048, 2048], P(None, 'ep'), may hold values from -0.125 to 0.125
- doc_start: int32 [16384], P('dp'), may hold values from 0 to 510, as said below
Outputs:
- gate_grad: bfloat16 [16384, 8], P(('dp', 'ep'))
- grad_gate_w: bfloat16 [128, 2048, 512], P(('ep', 'dp'))
- grad_up_w: bfloat16 [128, 2048, 512], P(('ep', 'dp'))
- grad_down_w: bfloat16 [128, 512, 2048], P(('ep', 'dp'))
- residual_grad: bfloat16 [16384, 2048], P(('dp', 'ep'))
- out_weight_grad: bfloat16 [2048, 2048], P('dp', 'ep')
- query_grad: bfloat16 [16384, 2048], P('dp', 'ep')
- key_grad: bfloat16 [16384, 2048], P('dp', 'ep')
- value_grad: bfloat16 [16384, 2048], P('dp', 'ep')
The draws below stay inside these ranges and needn't reach their ends.
Inputs may be any that keep to these rules, and one draw needn't show every extreme that they name: `expert_ids`: each token names 8 different experts; among the 128 rows of one device (aligned blocks of rows) no expert is named more than 10 times, and in some block some expert exactly 10 times. doc_start of a token is at most its own position in its sequence and equals that of the token before it unless a new document begins there; every document after the first holds two or more tokens.
All inputs are finite; a program needn't handle non-finite values.
Results may differ from the reference program's by a relative error of at most 0.019.
Values may be sent and summed in bfloat16 or wider, within the bound.
A program may use at most 192 MiB of HBM per device.

```python
import math
import jax
import jax.numpy as jnp
import numpy as np
from jax import lax

D = 2048
FF = 512
HEADS = 16
HEAD_DIM = 128
TOP = 8
SEQ = 512
EXPERTS = 128
TOKENS = 16384
TOK_DEV = 128
CAPS = 10
HHD = 2048


def doc_begins(key):
    seq_count = TOKENS // SEQ
    dice_rolls = jax.random.randint(jax.random.fold_in(key, 7), (seq_count, SEQ), 0, 48)
    positions = jnp.arange(SEQ, dtype=jnp.int32)[None, :]
    first_seq = jnp.arange(seq_count, dtype=jnp.int32)[:, None] == 0
    boundary = (dice_rolls == 0) & (positions >= 1) & (positions <= SEQ - 2)
    boundary = (boundary | first_seq & (positions == SEQ - 2)) & jnp.logical_not(first_seq & (positions == SEQ - 3))
    before = jnp.concatenate([jnp.zeros((seq_count, 1), dtype=jnp.bool_), boundary[:, :-1]], axis=1)
    boundary = boundary & jnp.logical_not(before)
    begins = jnp.where(boundary, positions, 0)
    return lax.cummax(begins, axis=1).astype(jnp.int32)


def draw_doc_start(key, part):
    return doc_begins(key).reshape(TOKENS)


def query_like(key, salt):
    seq_count = TOKENS // SEQ
    col_width = HEADS * HEAD_DIM
    values_base = jnp.clip(jax.random.normal(jax.random.fold_in(key, salt), (seq_count, SEQ, col_width), jnp.float32), -6.0, 6.0)
    return values_base.reshape(TOKENS, col_width).astype(jnp.bfloat16)


def draw_queries(key, part):
    return query_like(key, 1)


def draw_keys(key, part):
    return query_like(key, 2)


def shard_levels(own_key, extent, cuts, low, largest):
    gain, own = 1.0, jax.random.fold_in(own_key, 6)
    for dim, parts in cuts:
        draws = jnp.exp(jax.random.uniform(jax.random.fold_in(own, dim), (parts,), jnp.float32, low / len(cuts), largest / len(cuts)))
        gain = gain * jnp.repeat(draws, extent[dim] // parts).reshape([-1 if axis == dim else 1 for axis in range(len(extent))])
    return gain


def shared_out(own_key, own, number, rows, number_of, top, bound, lean):
    order = jax.random.permutation(own_key, number_of)
    heavy_load, ordinary = shares(number_of, rows * top, bound, lean, True), shares(number_of, rows * top, bound, lean, False)
    places = jnp.arange(number_of)

    def named(sizes, offset_by):
        used = int((sizes > 0).sum())
        fixed = max(1, used // 4)
        moved = fixed + (places - fixed + offset_by * (used - fixed)) % max(1, number_of - fixed)
        return jnp.zeros((number_of,), jnp.int32).at[order[jnp.where(places < fixed, places, moved)]].set(jnp.asarray(sizes, jnp.int32))

    sizes = jnp.where(number % 4 == 0, named(heavy_load, number // 4), named(ordinary, number - number // 4 - 1))
    mixed = jax.random.permutation(jax.random.fold_in(own, 3), number_of)
    giver, receiver = mixed[0:number_of // 2 * 2:2], mixed[1:number_of // 2 * 2:2]
    room = jnp.minimum(sizes[giver] - 1, bound - sizes[receiver]) // 2
    room = jnp.where((giver == order[0]) | (receiver == order[0]) | (sizes[receiver] == 0), 0, jnp.maximum(room, 0))
    moved = jax.random.randint(jax.random.fold_in(own, 4), (number_of // 2,), 0, 1 << 20) % (room + 1)
    sizes = sizes.at[giver].add(-moved).at[receiver].add(moved)
    items = jnp.searchsorted(jnp.cumsum(sizes), jnp.arange(rows * top), side="right").astype(jnp.int32)
    table = items.reshape(top, rows).T
    table = table[jax.random.permutation(jax.random.fold_in(own, 1), rows)]
    offset_by = jax.random.randint(jax.random.fold_in(own, 2), (rows, 1), 0, top)
    return jnp.take_along_axis(table, (jnp.arange(top)[None, :] + offset_by) % top, axis=1)


def shares(count, total, limit, slope, full):
    loads = [(1 << 20) // math.isqrt(grade ** slope) + 1 for grade in range(1, count + 1)]
    largest = limit if full else min(limit, max(-(-total // count), total * loads[0] // sum(loads)))
    least = 1 if total - largest >= count - 1 else 0
    counts, spare = [largest] + [least] * (count - 1), total - largest - least * (count - 1)
    while spare > 0:
        movable = [i for i in range(1, count) if counts[i] < largest] or [i for i in range(1, count) if counts[i] < limit]
        pool, budget = sum([loads[i] for i in movable]), spare
        for i in movable:
            more = min(limit - counts[i], max(1, budget * loads[i] // pool), spare)
            counts[i] = counts[i] + more
            spare = spare - more
    return np.array(counts)


def scatter_about(rng, dims, spread, bound, pieces=(), held_as=jnp.bfloat16):
    loudness = shard_levels(rng, dims, pieces, -0.22, 0.18) if pieces else 1.0
    drawn = jax.random.normal(rng, dims, jnp.float32) * spread * loudness
    return jnp.minimum(jnp.maximum(drawn, -bound), bound).astype(held_as)


def setup_inputs(seed: int = 0) -> dict:
    seeds = jax.random.split(jax.random.key(seed), 15)
    hidden_state = scatter_about(seeds[0], (TOKENS, D), 1.0, 6.0, ((0, 128),))
    out_grad = scatter_about(seeds[1], (TOKENS, D), 1.0, 6.0, ((0, 128),))
    norm_gain = jnp.clip(1.0 + 0.1 * jax.random.normal(seeds[2], (D,), jnp.float32), 0.5, 1.5).astype(jnp.bfloat16)
    expert_ids_keys = jax.random.split(jax.random.fold_in(seeds[3], 1), TOKENS // TOK_DEV)
    expert_ids_turns = jax.random.permutation(jax.random.fold_in(seeds[3], 3), TOKENS // TOK_DEV)
    expert_ids = jax.vmap(lambda own, number: shared_out(jax.random.fold_in(seeds[3], 2), own, number, TOK_DEV, EXPERTS, TOP, CAPS, 2))(expert_ids_keys, expert_ids_turns).reshape((TOKENS, TOP))
    route_weight = jnp.clip(jnp.exp(math.log(0.3984375) - 2.9969585 * jax.random.uniform(seeds[4], (TOKENS, TOP), jnp.float32) ** shard_levels(seeds[4], (TOKENS, TOP), ((0, 128),), -0.2, 0.2)), 0.019897461, 0.3984375).astype(jnp.bfloat16)
    w_gate = scatter_about(seeds[5], (EXPERTS, D, FF), D ** -0.5, 0.125, ((0, 128),))
    w_up = scatter_about(seeds[6], (EXPERTS, D, FF), D ** -0.5, 0.125, ((0, 128),))
    w_down = scatter_about(seeds[7], (EXPERTS, FF, D), FF ** -0.5, 0.25, ((0, 128),))
    queries = draw_queries(jax.random.fold_in(seeds[14], 71), 0)
    keys = draw_keys(jax.random.fold_in(seeds[14], 71), 0)
    values = scatter_about(seeds[10], (TOKENS, HHD), 1.0, 6.0, ((0, 16), (1, 8)))
    attn_out = scatter_about(seeds[11], (TOKENS, HHD), 0.5, 4.0, ((0, 16), (1, 8)))
    out_weight = scatter_about(seeds[12], (D, HHD), HHD ** -0.5, 0.125, ((1, 8),))
    doc_start = draw_doc_start(jax.random.fold_in(seeds[14], 71), 0)
    return dict(hidden_state=hidden_state, out_grad=out_grad, norm_gain=norm_gain, expert_ids=expert_ids, route_weight=route_weight, w_gate=w_gate, w_up=w_up, w_down=w_down, queries=queries, keys=keys, values=values, attn_out=attn_out, out_weight=out_weight, doc_start=doc_start)


EPS = 1e-06

def reference(hidden_state, out_grad, norm_gain, expert_ids, route_weight, w_gate, w_up, w_down, queries, keys, values, attn_out, out_weight, doc_start):
    hidden_f32 = hidden_state.astype(jnp.float32)
    inv_rms = lax.rsqrt(lax.optimization_barrier(jnp.mean(hidden_f32 * hidden_f32, axis=1, keepdims=True)) + EPS)
    unit_hidden = hidden_f32 * inv_rms
    gain_f32 = norm_gain.astype(jnp.float32)
    normed = (unit_hidden * gain_f32).astype(jnp.bfloat16)
    block_count = TOKENS // TOK_DEV
    pair_count = TOKENS * TOP
    block_ids = expert_ids.reshape(block_count, TOK_DEV * TOP)
    one_hot = (block_ids[:, :, None] == jnp.arange(EXPERTS, dtype=jnp.int32)[None, None, :]).astype(jnp.int32)
    earlier = lax.optimization_barrier(jnp.sum((jnp.cumsum(one_hot, axis=1) - one_hot) * one_hot, axis=2))
    slot_place = (jnp.arange(block_count, dtype=jnp.int32)[:, None] * CAPS + earlier).reshape(pair_count).astype(jnp.int32)
    table = jnp.full((EXPERTS, block_count * CAPS), pair_count, dtype=jnp.int32)
    table = table.at[expert_ids.reshape(pair_count), slot_place].set(jnp.arange(pair_count, dtype=jnp.int32))
    zero_row = jnp.zeros((1, D), dtype=jnp.bfloat16)
    normed_pad = jnp.concatenate([normed, zero_row], axis=0)
    grad_pad = jnp.concatenate([out_grad, zero_row], axis=0)
    weight_pad = jnp.concatenate([route_weight.reshape(pair_count), jnp.zeros((1,), dtype=jnp.bfloat16)])
    grad_scale = (TOK_DEV * TOP) ** (-0.5)
    out_scale = D ** (-0.5)

    def expert_step(carry, inputs):
        normed_grad, gate_scores = carry
        pair_index, gate_mat, up_mat, down_mat = inputs
        token_index = pair_index // TOP
        rows_in = normed_pad[token_index]
        rows_grad = grad_pad[token_index]
        rows_weight = weight_pad[pair_index].astype(jnp.float32)[:, None]
        gate_pre = jnp.dot(rows_in, gate_mat, preferred_element_type=jnp.float32)
        up_proj = jnp.dot(rows_in, up_mat, preferred_element_type=jnp.float32)
        sigmoid_gate = jax.nn.sigmoid(gate_pre)
        act_bf16 = (gate_pre * sigmoid_gate * up_proj).astype(jnp.bfloat16)
        expert_out = jnp.dot(act_bf16, down_mat, preferred_element_type=jnp.float32)
        gate_score = (lax.optimization_barrier(jnp.sum(rows_grad.astype(jnp.float32) * expert_out, axis=1)) * out_scale).astype(jnp.bfloat16)
        scaled_grad = (rows_weight * rows_grad.astype(jnp.float32)).astype(jnp.bfloat16)
        act_grad = jnp.dot(scaled_grad, down_mat.T, preferred_element_type=jnp.float32)
        pre_grad = (act_grad * up_proj * sigmoid_gate * (1.0 + gate_pre * (1.0 - sigmoid_gate))).astype(jnp.bfloat16)
        up_grad = (act_grad * gate_pre * sigmoid_gate).astype(jnp.bfloat16)
        row_grad = (jnp.dot(pre_grad, gate_mat.T, preferred_element_type=jnp.float32) + jnp.dot(up_grad, up_mat.T, preferred_element_type=jnp.float32)).astype(jnp.bfloat16)
        gate_part = (jnp.dot(rows_in.T, pre_grad, preferred_element_type=jnp.float32) * grad_scale).astype(jnp.bfloat16)
        up_part = (jnp.dot(rows_in.T, up_grad, preferred_element_type=jnp.float32) * grad_scale).astype(jnp.bfloat16)
        down_part = (jnp.dot(act_bf16.T, scaled_grad, preferred_element_type=jnp.float32) * grad_scale).astype(jnp.bfloat16)
        normed_grad = normed_grad.at[token_index].add(row_grad.astype(jnp.float32))
        gate_scores = gate_scores.at[pair_index].set(gate_score)
        return ((normed_grad, gate_scores), (gate_part, up_part, down_part))
    start_carry = (jnp.zeros((TOKENS + 1, D), dtype=jnp.float32), jnp.zeros((pair_count + 1,), dtype=jnp.bfloat16))
    (normed_grad, gate_scores), (grad_gate_w, grad_up_w, grad_down_w) = lax.scan(expert_step, start_carry, (table, w_gate, w_up, w_down))
    normed_grad = normed_grad[:TOKENS]
    gate_grad = gate_scores[:pair_count].reshape(TOKENS, TOP)
    scaled_norm = normed_grad * gain_f32
    residual_f32 = out_grad.astype(jnp.float32) + inv_rms * (scaled_norm - unit_hidden * lax.optimization_barrier(jnp.mean(scaled_norm * unit_hidden, axis=1, keepdims=True)))
    residual_grad = residual_f32.astype(jnp.bfloat16)
    attn_grad = jnp.dot(residual_grad, out_weight, preferred_element_type=jnp.float32).astype(jnp.bfloat16)
    out_weight_grad = (jnp.dot(residual_grad.T, attn_out, preferred_element_type=jnp.float32) * TOKENS ** (-0.5)).astype(jnp.bfloat16)
    seq_count = TOKENS // SEQ

    def heads_view(array):
        return array.reshape(seq_count, SEQ, HEADS, HEAD_DIM)
    score_scale = HEAD_DIM ** (-0.5)

    def one_sequence(inputs):
        query_rows, key_rows, value_rows, output_rows, grad_rows, begins = inputs
        positions = jnp.arange(SEQ, dtype=jnp.int32)
        visible = (positions[None, :] <= positions[:, None]) & (positions[None, :] >= begins[:, None])
        scores = jnp.einsum('qhd,khd->hqk', query_rows.astype(jnp.float32), key_rows.astype(jnp.float32)) * score_scale
        masked = jnp.where(visible[None], scores, -1e+30)
        top_score = lax.optimization_barrier(jnp.max(masked, axis=2, keepdims=True))
        weights = jnp.where(visible[None], jnp.exp(masked - top_score), 0.0)
        probs = weights / lax.optimization_barrier(jnp.sum(weights, axis=2, keepdims=True))
        probs_bf16 = probs.astype(jnp.bfloat16)
        delta = lax.optimization_barrier(jnp.sum(grad_rows.astype(jnp.float32) * output_rows.astype(jnp.float32), axis=2)).T
        prob_grad = jnp.einsum('qhd,khd->hqk', grad_rows.astype(jnp.float32), value_rows.astype(jnp.float32))
        score_grad = (probs * (prob_grad - delta[:, :, None])).astype(jnp.bfloat16)
        query_part = (jnp.einsum('hqk,khd->qhd', score_grad.astype(jnp.float32), key_rows.astype(jnp.float32)) * score_scale).astype(jnp.bfloat16)
        key_part = (jnp.einsum('hqk,qhd->khd', score_grad.astype(jnp.float32), query_rows.astype(jnp.float32)) * score_scale).astype(jnp.bfloat16)
        value_part = jnp.einsum('hqk,qhd->khd', probs_bf16.astype(jnp.float32), grad_rows.astype(jnp.float32)).astype(jnp.bfloat16)
        return (query_part, key_part, value_part)
    query_grad, key_grad, value_grad = lax.map(one_sequence, (heads_view(queries), heads_view(keys), heads_view(values), heads_view(attn_out), heads_view(attn_grad), doc_start.reshape(seq_count, SEQ)))
    query_grad = query_grad.reshape(TOKENS, HHD)
    key_grad = key_grad.reshape(TOKENS, HHD)
    value_grad = value_grad.reshape(TOKENS, HHD)
    return (gate_grad, grad_gate_w, grad_up_w, grad_down_w, residual_grad, out_weight_grad, query_grad, key_grad, value_grad)
```

```python
import functools

import jax
import jax.numpy as jnp
import numpy as np
from jax import lax
from jax.experimental import pallas as pl
from jax.experimental.pallas import tpu as pltpu
from jax.sharding import PartitionSpec as P

HEAD_DIM = 128
SEQ = 512
EPS = 1e-06
LANES = 128
CHUNKS = 16
F32 = jnp.float32
BF16 = jnp.bfloat16
LAST = (((1,), (1,)), ((), ()))
FIRST = (((0,), (0,)), ((), ()))
PACK_EXTRA = 8
VMEM_LIMIT = 56 * 1024 * 1024


def swap_matrix():
    index = np.arange(256)
    matrix = np.zeros((256, 256), np.float32)
    matrix[(index % 16) * 16 + index // 16, index] = 1.0
    return jnp.asarray(matrix, BF16)


def call(kernel, out_shape, flops=0, moved=0, **kwargs):
    return pl.pallas_call(
        kernel,
        out_shape=out_shape,
        compiler_params=pltpu.CompilerParams(vmem_limit_bytes=VMEM_LIMIT),
        cost_estimate=pl.CostEstimate(flops=flops, bytes_accessed=moved, transcendentals=0),
        **kwargs,
    )


def whole(shape):
    return pl.BlockSpec(shape, lambda *_: (0,) * len(shape))


def tiles_to_rows(get_tiles, swap, out_ref, groups):
    for group in range(groups):
        pair = jnp.concatenate([get_tiles(2 * group), get_tiles(2 * group + 1)], axis=1)
        turned = jnp.dot(swap, pair, preferred_element_type=F32).astype(BF16)
        for chunk in range(CHUNKS):
            cols = slice(chunk * LANES, (chunk + 1) * LANES)
            rows = turned[chunk * 16 : (chunk + 1) * 16]
            out_ref[group * 32 : group * 32 + 16, cols] = rows[:, :LANES]
            out_ref[group * 32 + 16 : group * 32 + 32, cols] = rows[:, LANES:]


def slots_kernel(caps, ids_ref, weight_ref, table_ref, scale_ref, slot_ref):
    tokens, top_k = ids_ref.shape
    experts = LANES
    lane = lax.broadcasted_iota(jnp.int32, (tokens, experts), 1)
    row = lax.broadcasted_iota(jnp.int32, (tokens, experts), 0)
    ids = ids_ref[...]
    weight = weight_ref[...].astype(F32)
    chosen = jnp.zeros((tokens, experts), F32)
    weights = jnp.zeros((tokens, experts), F32)
    for k in range(top_k):
        hit = ids[:, k : k + 1] == lane
        chosen = jnp.where(hit, 1.0, chosen)
        weights = jnp.where(hit, weight[:, k : k + 1], weights)
    lower = jnp.where(lane < row, 1.0, 0.0).astype(BF16)
    counts = jnp.dot(lower, chosen.astype(BF16), preferred_element_type=F32)
    table = jnp.zeros((16, experts), F32)
    scales = jnp.zeros((16, experts), F32)
    sub = lax.broadcasted_iota(jnp.int32, (16, experts), 0)
    from_end = (row - tokens).astype(F32)
    for place in range(caps):
        mask = (chosen > 0.5) & (jnp.abs(counts - place) < 0.5)
        token = jnp.sum(jnp.where(mask, from_end, 0.0), axis=0, keepdims=True) + tokens
        scale = jnp.sum(jnp.where(mask, weights, 0.0), axis=0, keepdims=True)
        table = jnp.where(sub == place, token, table)
        scales = jnp.where(sub == place, scale, scales)
    table_ref[...] = table.astype(jnp.int32)
    scale_ref[...] = scales
    slot = jnp.zeros((tokens, experts), F32)
    for k in range(top_k):
        place = jnp.sum(jnp.where(ids[:, k : k + 1] == lane, counts, 0.0), axis=1, keepdims=True)
        slot = jnp.where(lane == k, place, slot)
    slot_ref[...] = slot.astype(jnp.int32)


def pack_rows_kernel(caps, table_ref, hidden_ref, gain_ref, out_ref, normed):
    tokens = hidden_ref.shape[0]
    step = pl.program_id(0)

    @pl.when(step == 0)
    def _():
        gain = gain_ref[...].astype(F32)[None]
        for start in range(0, tokens, 16):
            hidden = hidden_ref[start : start + 16].astype(F32)
            mean = jnp.sum(
                jnp.sum(hidden * hidden, axis=2, keepdims=True), axis=1, keepdims=True
            ) * (1.0 / (CHUNKS * LANES))
            normed[start : start + 16] = (hidden * lax.rsqrt(mean + EPS) * gain).astype(BF16)
        normed[tokens] = jnp.zeros((CHUNKS, LANES), BF16)

    def fill(dest, carry):
        for place in range(caps):
            out_ref[dest * caps + place] = normed[table_ref[place, step * 16 + dest]]
        return carry

    lax.fori_loop(0, 16, fill, 0)


def pack_grads_kernel(caps, table_ref, scale_ref, grad_ref, out_ref):
    tokens = grad_ref.shape[0]
    step = pl.program_id(0)

    def fill(dest, carry):
        for place in range(caps):
            token = jnp.minimum(table_ref[place, step * 16 + dest], tokens - 1)
            scale = scale_ref[place, step * 16 + dest]
            out_ref[dest * caps + place] = (grad_ref[token].astype(F32) * scale).astype(BF16)
        return carry

    lax.fori_loop(0, 16, fill, 0)


def expert_up_kernel(tile_ref, swap_ref, gate_w_ref, up_w_ref, row_ref, act_ref, da_ref, db_ref):
    rows = row_ref.shape[0]
    tiles_to_rows(
        lambda i: tile_ref[i * 256 : (i + 1) * 256], swap_ref[...], row_ref, rows // 32
    )
    gate = jnp.dot(row_ref[...], gate_w_ref[0], preferred_element_type=F32)
    up = jnp.dot(row_ref[...], up_w_ref[0], preferred_element_type=F32)
    sig = 1.0 / (1.0 + jnp.exp(-gate))
    silu = gate * sig
    act_ref[...] = (silu * up).astype(BF16)
    da_ref[...] = (up * sig * (1.0 + gate * (1.0 - sig))).astype(BF16)
    db_ref[...] = silu.astype(BF16)


def expert_down_kernel(
    caps,
    tile_ref,
    swap_ref,
    gather_ref,
    spread_ref,
    gate_w_ref,
    up_w_ref,
    down_w_ref,
    act_ref,
    da_ref,
    db_ref,
    grad_ref,
    pre_ref,
    upg_ref,
    back_ref,
    rowg,
):
    rows = grad_ref.shape[0]
    swap = swap_ref[...]
    tiles_to_rows(lambda i: tile_ref[i * 256 : (i + 1) * 256], swap, grad_ref, rows // 32)
    act_grad = lax.dot_general(grad_ref[...], down_w_ref[0], LAST, preferred_element_type=F32)
    pre = (act_grad * da_ref[...].astype(F32)).astype(BF16)
    upg = (act_grad * db_ref[...].astype(F32)).astype(BF16)
    pre_ref[...] = pre
    upg_ref[...] = upg
    score = jnp.sum(act_grad * act_ref[...].astype(F32), axis=1, keepdims=True)
    placed = jnp.dot(
        gather_ref[...],
        (score * spread_ref[...].astype(F32)).astype(BF16),
        preferred_element_type=F32,
    ).astype(BF16)
    rowg[...] = (
        lax.dot_general(pre, gate_w_ref[0], LAST, preferred_element_type=F32)
        + lax.dot_general(upg, up_w_ref[0], LAST, preferred_element_type=F32)
    ).astype(BF16)
    for group in range(rows // 32):
        halves = []
        for half in range(2):
            at = group * 32 + half * 16
            halves.append(
                jnp.concatenate(
                    [
                        rowg[at : at + 16, chunk * LANES : (chunk + 1) * LANES]
                        for chunk in range(CHUNKS)
                    ],
                    axis=0,
                )
            )
        turned = jnp.dot(
            swap, jnp.concatenate(halves, axis=1), preferred_element_type=F32
        ).astype(BF16)
        for half in range(2):
            for inner in range(16):
                row = group * 32 + half * 16 + inner
                place = (row % caps) * 16
                back_ref[row // caps, place : place + 16, :] = turned[
                    inner * 16 : (inner + 1) * 16, half * LANES : (half + 1) * LANES
                ]
    for source in range(rows // caps):
        back_ref[source, caps * 16 : caps * 16 + PACK_EXTRA, :] = jnp.broadcast_to(
            placed[source : source + 1], (PACK_EXTRA, LANES)
        )


def combine_kernel(
    ids_ref, slot_ref, back_ref, hidden_ref, grad_ref, gain_ref, swap_ref, out_ref, total, tiles
):
    tokens = hidden_ref.shape[0]
    top_k = ids_ref.shape[1]

    def gather(token, carry):
        acc = jnp.zeros((CHUNKS, LANES), F32)
        for k in range(top_k):
            at = pl.multiple_of(slot_ref[token, k] * 16, 16)
            acc = acc + back_ref[ids_ref[token, k], pl.ds(at, 16), :].astype(F32)
        total[token] = acc
        return carry

    lax.fori_loop(0, tokens, gather, 0, unroll=2)
    gain = gain_ref[...].astype(F32)[None]
    share = 1.0 / (CHUNKS * LANES)

    def mean(value):
        return (
            jnp.sum(jnp.sum(value, axis=2, keepdims=True), axis=1, keepdims=True) * share
        )

    for start in range(0, tokens, 16):
        hidden = hidden_ref[start : start + 16].astype(F32)
        inv_rms = lax.rsqrt(mean(hidden * hidden) + EPS)
        unit = hidden * inv_rms
        scaled = total[start : start + 16] * gain
        residual = grad_ref[start : start + 16].astype(F32) + inv_rms * (
            scaled - unit * mean(scaled * unit)
        )
        tiles[start * 16 : start * 16 + 256] = residual.astype(BF16).reshape(256, LANES)
    tiles_to_rows(
        lambda i: tiles[i * 256 : (i + 1) * 256], swap_ref[...], out_ref, tokens // 32
    )


def gate_kernel(ids_ref, slot_ref, weight_ref, score_ref, out_ref):
    tokens, top_k = ids_ref.shape
    lane = lax.broadcasted_iota(jnp.int32, (tokens, LANES), 1)
    ids = ids_ref[...]
    slot = slot_ref[...]
    found = jnp.zeros((tokens, LANES), F32)
    for k in range(top_k):
        hit = jnp.where(ids[:, k : k + 1] == lane, 1.0, 0.0).astype(BF16)
        mine = jnp.dot(hit, score_ref[...], preferred_element_type=F32)
        value = jnp.sum(jnp.where(slot[:, k : k + 1] == lane, mine, 0.0), axis=1, keepdims=True)
        found = jnp.where(lane == k, value, found)
    scale = (CHUNKS * LANES) ** (-0.5)
    out_ref[...] = (found[:, :top_k] * scale / weight_ref[...].astype(F32)).astype(BF16)


def probs_kernel(query_ref, key_ref, begin_ref, out_ref):
    scores = lax.dot_general(
        query_ref[...], key_ref[...], LAST, preferred_element_type=F32
    ) * HEAD_DIM ** (-0.5)
    here = lax.broadcasted_iota(jnp.int32, (SEQ, SEQ), 0)
    there = lax.broadcasted_iota(jnp.int32, (SEQ, SEQ), 1)
    visible = (there <= here) & (there >= begin_ref[...])
    masked = jnp.where(visible, scores, -1e30)
    top = jnp.max(masked, axis=1, keepdims=True)
    weights = jnp.where(visible, jnp.exp(masked - top), 0.0)
    out_ref[0, 0] = (weights / jnp.sum(weights, axis=1, keepdims=True)).astype(BF16)


def attention_kernel(
    probs_ref, query_ref, key_ref, value_ref, attn_ref, grad_ref, dq_ref, dk_ref, dv_ref
):
    probs = probs_ref[0, 0]
    grad = grad_ref[...]
    delta = jnp.sum(grad.astype(F32) * attn_ref[...].astype(F32), axis=1, keepdims=True)
    prob_grad = lax.dot_general(grad, value_ref[...], LAST, preferred_element_type=F32)
    score_grad = (probs.astype(F32) * (prob_grad - delta)).astype(BF16)
    scale = HEAD_DIM ** (-0.5)
    dq_ref[...] = (
        jnp.dot(score_grad, key_ref[...], preferred_element_type=F32) * scale
    ).astype(BF16)
    dk_ref[...] = (
        lax.dot_general(score_grad, query_ref[...], FIRST, preferred_element_type=F32) * scale
    ).astype(BF16)
    dv_ref[...] = lax.dot_general(probs, grad, FIRST, preferred_element_type=F32).astype(BF16)


def per_device(
    hidden_state,
    out_grad,
    norm_gain,
    expert_ids,
    route_weight,
    w_gate,
    w_up,
    w_down,
    queries,
    keys,
    values,
    attn_out,
    out_weight,
    doc_start,
):
    tokens, width = hidden_state.shape
    top_k = expert_ids.shape[1]
    ff = w_gate.shape[2]
    dp_size = lax.axis_size("dp")
    experts = lax.axis_size("ep") * dp_size
    caps = 5 * tokens * top_k // (4 * experts)
    rows = experts * caps
    both = ("ep", "dp")
    swap = swap_matrix()
    hidden3 = hidden_state.reshape(tokens, CHUNKS, LANES)
    grad3 = out_grad.reshape(tokens, CHUNKS, LANES)
    gain2 = norm_gain.reshape(CHUNKS, LANES)

    table, scales, slots = call(
        functools.partial(slots_kernel, caps),
        (
            jax.ShapeDtypeStruct((16, LANES), jnp.int32),
            jax.ShapeDtypeStruct((16, LANES), F32),
            jax.ShapeDtypeStruct((tokens, LANES), jnp.int32),
        ),
        moved=300000,
    )(expert_ids, route_weight)

    step_rows = 16 * caps
    steps = rows // step_rows
    tile_block = pl.BlockSpec((step_rows, CHUNKS, LANES), lambda i, *_: (i, 0, 0))
    send_rows = call(
        functools.partial(pack_rows_kernel, caps),
        jax.ShapeDtypeStruct((rows, CHUNKS, LANES), BF16),
        moved=12000000,
        grid_spec=pltpu.PrefetchScalarGridSpec(
            num_scalar_prefetch=1,
            grid=(steps,),
            in_specs=[whole((tokens, CHUNKS, LANES)), whole((CHUNKS, LANES))],
            out_specs=tile_block,
            scratch_shapes=[pltpu.VMEM((tokens + 1, CHUNKS, LANES), BF16)],
        ),
    )(table, hidden3, gain2)
    send_grads = call(
        functools.partial(pack_grads_kernel, caps),
        jax.ShapeDtypeStruct((rows, CHUNKS, LANES), BF16),
        moved=12000000,
        grid_spec=pltpu.PrefetchScalarGridSpec(
            num_scalar_prefetch=2,
            grid=(steps,),
            in_specs=[whole((tokens, CHUNKS, LANES))],
            out_specs=tile_block,
        ),
    )(table, scales, grad3)

    def exchange(array):
        return lax.all_to_all(array, both, split_axis=0, concat_axis=0, tiled=True)

    got_rows = exchange(send_rows.reshape(experts, caps * 16, LANES)).reshape(rows * 16, LANES)
    got_grads = exchange(send_grads.reshape(experts, caps * 16, LANES)).reshape(rows * 16, LANES)

    group_len, head_cols = queries.shape
    head_count = head_cols // HEAD_DIM
    seq_count = group_len // SEQ
    head_block = pl.BlockSpec((SEQ, HEAD_DIM), lambda s, h: (s, h))
    probs_block = pl.BlockSpec((1, 1, SEQ, SEQ), lambda s, h: (s, h, 0, 0))
    probs = call(
        probs_kernel,
        jax.ShapeDtypeStruct((seq_count, head_count, SEQ, SEQ), BF16),
        flops=10**10,
        moved=5000000,
        grid=(seq_count, head_count),
        in_specs=[head_block, head_block, pl.BlockSpec((SEQ, 1), lambda s, h: (s, 0))],
        out_specs=probs_block,
    )(queries, keys, doc_start.reshape(group_len, 1))

    flat_tiles = pl.BlockSpec((step_rows * 16, LANES), lambda i: (i, 0))
    wide = pl.BlockSpec((step_rows, width), lambda i: (i, 0))
    narrow = pl.BlockSpec((step_rows, ff), lambda i: (i, 0))
    w_in = whole((1, width, ff))
    w_out = whole((1, ff, width))
    narrow_shape = jax.ShapeDtypeStruct((rows, ff), BF16)
    wide_shape = jax.ShapeDtypeStruct((rows, width), BF16)
    rows_in, act, act_da, act_db = call(
        expert_up_kernel,
        (wide_shape, narrow_shape, narrow_shape, narrow_shape),
        flops=4 * rows * width * ff,
        moved=18000000,
        grid=(steps,),
        in_specs=[flat_tiles, whole((256, 256)), w_in, w_in],
        out_specs=(wide, narrow, narrow, narrow),
    )(got_rows, swap, w_gate, w_up)
    index = np.arange(step_rows)
    gather = jnp.asarray(index[None, :] // caps == np.arange(16)[:, None], BF16)
    spread = jnp.asarray(index[:, None] % caps == np.arange(LANES)[None, :], BF16)
    block_rows = caps * 16 + PACK_EXTRA
    scaled_grad, pre_grad, up_grad, send_back = call(
        functools.partial(expert_down_kernel, caps),
        (
            wide_shape,
            narrow_shape,
            narrow_shape,
            jax.ShapeDtypeStruct((experts, block_rows, LANES), BF16),
        ),
        flops=6 * rows * width * ff,
        moved=25000000,
        grid=(steps,),
        in_specs=[
            flat_tiles,
            whole((256, 256)),
            whole((16, step_rows)),
            whole((step_rows, LANES)),
            w_in,
            w_in,
            w_out,
            narrow,
            narrow,
            narrow,
        ],
        out_specs=(
            wide,
            narrow,
            narrow,
            pl.BlockSpec((16, block_rows, LANES), lambda i: (i, 0, 0)),
        ),
        scratch_shapes=[pltpu.VMEM((step_rows, width), BF16)],
    )(got_grads, swap, gather, spread, w_gate, w_up, w_down, act, act_da, act_db)
    back = exchange(send_back)
    grad_scale = (tokens * top_k) ** (-0.5)

    def weight_grad(left, right):
        product = lax.dot_general(left, right, FIRST, preferred_element_type=F32)
        return (product * grad_scale).astype(BF16)[None]

    grad_gate_w = weight_grad(rows_in, pre_grad)
    grad_up_w = weight_grad(rows_in, up_grad)
    grad_down_w = weight_grad(act, scaled_grad)

    residual_grad = call(
        combine_kernel,
        jax.ShapeDtypeStruct((tokens, width), BF16),
        moved=8000000,
        grid_spec=pltpu.PrefetchScalarGridSpec(
            num_scalar_prefetch=2,
            grid=(1,),
            in_specs=[
                whole((experts, block_rows, LANES)),
                whole((tokens, CHUNKS, LANES)),
                whole((tokens, CHUNKS, LANES)),
                whole((CHUNKS, LANES)),
                whole((256, 256)),
            ],
            out_specs=whole((tokens, width)),
            scratch_shapes=[
                pltpu.VMEM((tokens, CHUNKS, LANES), F32),
                pltpu.VMEM((tokens * CHUNKS, LANES), BF16),
            ],
        ),
    )(expert_ids, slots, back, hidden3, grad3, gain2, swap)
    gate_grad = call(gate_kernel, jax.ShapeDtypeStruct((tokens, top_k), BF16), moved=200000)(
        expert_ids, slots, route_weight, back[:, caps * 16, :]
    )

    group_rows = lax.all_gather(residual_grad, "ep", axis=0, tiled=True)
    partial_w = lax.dot_general(
        group_rows, attn_out, FIRST, preferred_element_type=F32
    ).astype(BF16)
    pieces = lax.all_to_all(
        partial_w.reshape(dp_size, width // dp_size, head_cols),
        "dp",
        split_axis=0,
        concat_axis=0,
        tiled=True,
    )
    out_weight_grad = (
        jnp.sum(pieces.astype(F32), axis=0) * (group_len * dp_size) ** (-0.5)
    ).astype(BF16)
    attn_grad = jnp.dot(group_rows, out_weight, preferred_element_type=F32).astype(BF16)
    head_shape = jax.ShapeDtypeStruct((group_len, head_cols), BF16)
    query_grad, key_grad, value_grad = call(
        attention_kernel,
        (head_shape, head_shape, head_shape),
        flops=4 * 8 * SEQ * SEQ * HEAD_DIM,
        moved=6000000,
        grid=(seq_count, head_count),
        in_specs=[probs_block] + [head_block] * 5,
        out_specs=(head_block, head_block, head_block),
    )(probs, queries, keys, values, attn_out, attn_grad)
    return (
        gate_grad,
        grad_gate_w,
        grad_up_w,
        grad_down_w,
        residual_grad,
        out_weight_grad,
        query_grad,
        key_grad,
        value_grad,
    )


def solution(mesh):
    tokens = P(("dp", "ep"), None)
    expert = P(("ep", "dp"), None, None)
    heads = P("dp", "ep")
    return jax.shard_map(
        per_device,
        mesh=mesh,
        in_specs=(
            tokens,
            tokens,
            P(),
            tokens,
            tokens,
            expert,
            expert,
            expert,
            heads,
            heads,
            heads,
            heads,
            P(None, "ep"),
            P("dp"),
        ),
        out_specs=(tokens, expert, expert, expert, tokens, heads, heads, heads, heads),
        check_vma=False,
    )
```

```python
import functools

import jax
import jax.numpy as jnp
import numpy as np
from jax import lax
from jax.experimental import pallas as pl
from jax.experimental.pallas import tpu as pltpu
from jax.sharding import PartitionSpec as P

HEAD_DIM = 128
SEQ = 512
EPS = 1e-06
LANES = 128
CHUNKS = 16
F32 = jnp.float32
BF16 = jnp.bfloat16
LAST = (((1,), (1,)), ((), ()))
FIRST = (((0,), (0,)), ((), ()))
PACK_EXTRA = 8
DESTS = 32
SOURCES = 32
VMEM_LIMIT = 56 * 1024 * 1024


def swap_matrix():
    index = np.arange(256)
    matrix = np.zeros((256, 256), np.float32)
    matrix[(index % 16) * 16 + index // 16, index] = 1.0
    return jnp.asarray(matrix, BF16)


def call(kernel, out_shape, flops=0, moved=0, **kwargs):
    return pl.pallas_call(
        kernel,
        out_shape=out_shape,
        compiler_params=pltpu.CompilerParams(vmem_limit_bytes=VMEM_LIMIT),
        cost_estimate=pl.CostEstimate(flops=flops, bytes_accessed=moved, transcendentals=0),
        **kwargs,
    )


def whole(shape):
    return pl.BlockSpec(shape, lambda *_: (0,) * len(shape))


def tiles_to_rows(get_tiles, swap, out_ref, groups):
    for group in range(groups):
        pair = jnp.concatenate([get_tiles(2 * group), get_tiles(2 * group + 1)], axis=1)
        turned = jnp.dot(swap, pair, preferred_element_type=F32).astype(BF16)
        for chunk in range(CHUNKS):
            cols = slice(chunk * LANES, (chunk + 1) * LANES)
            rows = turned[chunk * 16 : (chunk + 1) * 16]
            out_ref[group * 32 : group * 32 + 16, cols] = rows[:, :LANES]
            out_ref[group * 32 + 16 : group * 32 + 32, cols] = rows[:, LANES:]


def slots_kernel(caps, ids_ref, weight_ref, table_ref, scale_ref, slot_ref):
    top_k, tokens = ids_ref.shape
    experts = LANES
    lane = lax.broadcasted_iota(jnp.int32, (experts, tokens), 1)
    row = lax.broadcasted_iota(jnp.int32, (experts, tokens), 0)
    ids = ids_ref[...]
    weight = weight_ref[...].astype(F32)
    chosen = jnp.zeros((experts, tokens), F32)
    weights = jnp.zeros((experts, tokens), F32)
    for k in range(top_k):
        hit = ids[k : k + 1] == row
        chosen = jnp.where(hit, 1.0, chosen)
        weights = jnp.where(hit, weight[k : k + 1], weights)
    upper = jnp.where(row < lane, 1.0, 0.0).astype(BF16)
    counts = jnp.dot(chosen.astype(BF16), upper, preferred_element_type=F32)
    table = jnp.zeros((experts, LANES), F32)
    scales = jnp.zeros((experts, LANES), F32)
    from_end = (lane - tokens).astype(F32)
    for place in range(caps):
        mask = (chosen > 0.5) & (jnp.abs(counts - place) < 0.5)
        token = jnp.sum(jnp.where(mask, from_end, 0.0), axis=1, keepdims=True) + tokens
        scale = jnp.sum(jnp.where(mask, weights, 0.0), axis=1, keepdims=True)
        table = jnp.where(lane == place, token, table)
        scales = jnp.where(lane == place, scale, scales)
    table_ref[...] = table.astype(jnp.int32)
    scale_ref[...] = scales
    slot_ref[...] = jnp.concatenate(
        [
            jnp.sum(jnp.where(ids[k : k + 1] == row, counts, 0.0), axis=0, keepdims=True)
            for k in range(top_k)
        ],
        axis=0,
    ).astype(jnp.int32)


def pack_rows_kernel(table_ref, hidden_ref, gain_ref, out_ref, normed):
    tokens = hidden_ref.shape[0]
    step = pl.program_id(0)
    caps = out_ref.shape[0] // DESTS

    @pl.when(step == 0)
    def _():
        gain = gain_ref[...].astype(F32)[None]
        for start in range(0, tokens, 16):
            hidden = hidden_ref[start : start + 16].astype(F32)
            mean = jnp.sum(
                jnp.sum(hidden * hidden, axis=2, keepdims=True), axis=1, keepdims=True
            ) * (1.0 / (CHUNKS * LANES))
            normed[start : start + 16] = (hidden * lax.rsqrt(mean + EPS) * gain).astype(BF16)
        normed[tokens] = jnp.zeros((CHUNKS, LANES), BF16)

    def fill(dest, carry):
        for place in range(caps):
            out_ref[dest * caps + place] = normed[table_ref[step * DESTS + dest, place]]
        return carry

    lax.fori_loop(0, DESTS, fill, 0, unroll=2)


def pack_grads_kernel(table_ref, scale_ref, grad_ref, out_ref):
    tokens = grad_ref.shape[0]
    step = pl.program_id(0)
    caps = out_ref.shape[0] // DESTS

    def fill(dest, carry):
        for place in range(caps):
            at = step * DESTS + dest
            token = jnp.minimum(table_ref[at, place], tokens - 1)
            scale = scale_ref[at, place]
            out_ref[dest * caps + place] = (grad_ref[token].astype(F32) * scale).astype(BF16)
        return carry

    lax.fori_loop(0, DESTS, fill, 0, unroll=2)


def expert_up_kernel(tile_ref, swap_ref, gate_w_ref, up_w_ref, row_ref, act_ref, da_ref, db_ref):
    rows = row_ref.shape[0]
    tiles_to_rows(
        lambda i: tile_ref[i * 256 : (i + 1) * 256], swap_ref[...], row_ref, rows // 32
    )
    gate = jnp.dot(row_ref[...], gate_w_ref[0], preferred_element_type=F32)
    up = jnp.dot(row_ref[...], up_w_ref[0], preferred_element_type=F32)
    sig = 1.0 / (1.0 + jnp.exp(-gate))
    silu = gate * sig
    act_ref[...] = (silu * up).astype(BF16)
    da_ref[...] = (up * sig * (1.0 + gate * (1.0 - sig))).astype(BF16)
    db_ref[...] = silu.astype(BF16)


def expert_down_kernel(
    caps,
    tile_ref,
    swap_ref,
    gather_ref,
    spread_ref,
    gate_w_ref,
    up_w_ref,
    down_w_ref,
    act_ref,
    da_ref,
    db_ref,
    grad_ref,
    pre_ref,
    upg_ref,
    back_ref,
    rowg,
):
    rows = grad_ref.shape[0]
    swap = swap_ref[...]
    tiles_to_rows(lambda i: tile_ref[i * 256 : (i + 1) * 256], swap, grad_ref, rows // 32)
    act_grad = lax.dot_general(grad_ref[...], down_w_ref[0], LAST, preferred_element_type=F32)
    pre = (act_grad * da_ref[...].astype(F32)).astype(BF16)
    upg = (act_grad * db_ref[...].astype(F32)).astype(BF16)
    pre_ref[...] = pre
    upg_ref[...] = upg
    score = jnp.sum(act_grad * act_ref[...].astype(F32), axis=1, keepdims=True)
    placed = jnp.dot(
        gather_ref[...],
        (score * spread_ref[...].astype(F32)).astype(BF16),
        preferred_element_type=F32,
    ).astype(BF16)
    rowg[...] = (
        lax.dot_general(pre, gate_w_ref[0], LAST, preferred_element_type=F32)
        + lax.dot_general(upg, up_w_ref[0], LAST, preferred_element_type=F32)
    ).astype(BF16)
    for group in range(rows // 32):
        halves = []
        for side in range(2):
            at = group * 32 + side * 16
            halves.append(
                jnp.concatenate(
                    [
                        rowg[at : at + 16, chunk * LANES : (chunk + 1) * LANES]
                        for chunk in range(CHUNKS)
                    ],
                    axis=0,
                )
            )
        turned = jnp.dot(
            swap, jnp.concatenate(halves, axis=1), preferred_element_type=F32
        ).astype(BF16)
        for side in range(2):
            for inner in range(16):
                row = group * 32 + side * 16 + inner
                place = (row % caps) * 16
                back_ref[row // caps, place : place + 16, :] = turned[
                    inner * 16 : (inner + 1) * 16, side * LANES : (side + 1) * LANES
                ]
    for source in range(rows // caps):
        back_ref[source, caps * 16 : caps * 16 + PACK_EXTRA, :] = jnp.broadcast_to(
            placed[source : source + 1], (PACK_EXTRA, LANES)
        )


def combine_kernel(
    ids_ref, slot_ref, back_ref, hidden_ref, grad_ref, gain_ref, swap_ref, out_ref, total, tiles
):
    top_k, tokens = ids_ref.shape

    def gather(token, carry):
        acc = jnp.zeros((CHUNKS, LANES), F32)
        for k in range(top_k):
            at = pl.multiple_of(slot_ref[k, token] * 16, 16)
            acc = acc + back_ref[ids_ref[k, token], pl.ds(at, 16), :].astype(F32)
        total[token] = acc
        return carry

    lax.fori_loop(0, tokens, gather, 0, unroll=4)
    gain = gain_ref[...].astype(F32)[None]
    share = 1.0 / (CHUNKS * LANES)

    def mean(value):
        return (
            jnp.sum(jnp.sum(value, axis=2, keepdims=True), axis=1, keepdims=True) * share
        )

    for start in range(0, tokens, 16):
        hidden = hidden_ref[start : start + 16].astype(F32)
        inv_rms = lax.rsqrt(mean(hidden * hidden) + EPS)
        unit = hidden * inv_rms
        scaled = total[start : start + 16] * gain
        residual = grad_ref[start : start + 16].astype(F32) + inv_rms * (
            scaled - unit * mean(scaled * unit)
        )
        tiles[start * 16 : start * 16 + 256] = residual.astype(BF16).reshape(256, LANES)
    tiles_to_rows(
        lambda i: tiles[i * 256 : (i + 1) * 256], swap_ref[...], out_ref, tokens // 32
    )


def gate_kernel(ids_ref, slot_ref, weight_ref, score_ref, out_ref):
    top_k, tokens = ids_ref.shape
    row = lax.broadcasted_iota(jnp.int32, (LANES, tokens), 0)
    ids = ids_ref[...]
    slot = slot_ref[...]
    found = []
    for k in range(top_k):
        hit = jnp.where(ids[k : k + 1] == row, 1.0, 0.0).astype(BF16)
        mine = lax.dot_general(score_ref[...], hit, FIRST, preferred_element_type=F32)
        found.append(
            jnp.sum(jnp.where(slot[k : k + 1] == row, mine, 0.0), axis=0, keepdims=True)
        )
    scale = (CHUNKS * LANES) ** (-0.5)
    value = jnp.concatenate(found, axis=0) * scale / weight_ref[...].astype(F32)
    out_ref[...] = value.astype(BF16)


def probs_kernel(query_ref, key_ref, begin_ref, out_ref):
    scores = lax.dot_general(
        query_ref[...], key_ref[...], LAST, preferred_element_type=F32
    ) * HEAD_DIM ** (-0.5)
    here = lax.broadcasted_iota(jnp.int32, (SEQ, SEQ), 0)
    there = lax.broadcasted_iota(jnp.int32, (SEQ, SEQ), 1)
    visible = (there <= here) & (there >= begin_ref[...])
    masked = jnp.where(visible, scores, -1e30)
    top = jnp.max(masked, axis=1, keepdims=True)
    weights = jnp.where(visible, jnp.exp(masked - top), 0.0)
    out_ref[0, 0] = (weights / jnp.sum(weights, axis=1, keepdims=True)).astype(BF16)


def attention_kernel(
    probs_ref, query_ref, key_ref, value_ref, attn_ref, grad_ref, dq_ref, dk_ref, dv_ref
):
    probs = probs_ref[0, 0]
    grad = grad_ref[...]
    delta = jnp.sum(grad.astype(F32) * attn_ref[...].astype(F32), axis=1, keepdims=True)
    prob_grad = lax.dot_general(grad, value_ref[...], LAST, preferred_element_type=F32)
    score_grad = (probs.astype(F32) * (prob_grad - delta)).astype(BF16)
    scale = HEAD_DIM ** (-0.5)
    dq_ref[...] = (
        jnp.dot(score_grad, key_ref[...], preferred_element_type=F32) * scale
    ).astype(BF16)
    dk_ref[...] = (
        lax.dot_general(score_grad, query_ref[...], FIRST, preferred_element_type=F32) * scale
    ).astype(BF16)
    dv_ref[...] = lax.dot_general(probs, grad, FIRST, preferred_element_type=F32).astype(BF16)


def per_device(
    hidden_state,
    out_grad,
    norm_gain,
    expert_ids,
    route_weight,
    w_gate,
    w_up,
    w_down,
    queries,
    keys,
    values,
    attn_out,
    out_weight,
    doc_start,
):
    tokens, width = hidden_state.shape
    top_k = expert_ids.shape[1]
    ff = w_gate.shape[2]
    dp_size = lax.axis_size("dp")
    experts = lax.axis_size("ep") * dp_size
    caps = 5 * tokens * top_k // (4 * experts)
    rows = experts * caps
    both = ("ep", "dp")
    swap = swap_matrix()
    hidden3 = hidden_state.reshape(tokens, CHUNKS, LANES)
    grad3 = out_grad.reshape(tokens, CHUNKS, LANES)
    gain2 = norm_gain.reshape(CHUNKS, LANES)

    ids_t, weight_t = expert_ids.T, route_weight.T
    table, scales, slots = call(
        functools.partial(slots_kernel, caps),
        (
            jax.ShapeDtypeStruct((experts, LANES), jnp.int32),
            jax.ShapeDtypeStruct((experts, LANES), F32),
            jax.ShapeDtypeStruct((top_k, tokens), jnp.int32),
        ),
        moved=300000,
    )(ids_t, weight_t)

    pack_block = pl.BlockSpec((DESTS * caps, CHUNKS, LANES), lambda i, *_: (i, 0, 0))

    def exchange(array):
        return lax.all_to_all(array, both, split_axis=0, concat_axis=0, tiled=True)

    def send(kernel, scalars, arrays, scratch):
        packed = call(
            kernel,
            jax.ShapeDtypeStruct((rows, CHUNKS, LANES), BF16),
            moved=6000000,
            grid_spec=pltpu.PrefetchScalarGridSpec(
                num_scalar_prefetch=len(scalars),
                grid=(experts // DESTS,),
                in_specs=[whole(a.shape) for a in arrays],
                out_specs=pack_block,
                scratch_shapes=scratch,
            ),
        )(*scalars, *arrays)
        return exchange(packed.reshape(experts, caps * 16, LANES)).reshape(rows * 16, LANES)

    table_scratch = [pltpu.VMEM((tokens + 1, CHUNKS, LANES), BF16)]
    got_rows = send(pack_rows_kernel, [table], [hidden3, gain2], table_scratch)
    got_grads = send(pack_grads_kernel, [table, scales], [grad3], [])

    group_len, head_cols = queries.shape
    head_count = head_cols // HEAD_DIM
    seq_count = group_len // SEQ
    head_block = pl.BlockSpec((SEQ, HEAD_DIM), lambda s, h: (s, h))
    probs_block = pl.BlockSpec((1, 1, SEQ, SEQ), lambda s, h: (s, h, 0, 0))
    probs = call(
        probs_kernel,
        jax.ShapeDtypeStruct((seq_count, head_count, SEQ, SEQ), BF16),
        flops=10**10,
        moved=5000000,
        grid=(seq_count, head_count),
        in_specs=[head_block, head_block, pl.BlockSpec((SEQ, 1), lambda s, h: (s, 0))],
        out_specs=probs_block,
    )(queries, keys, doc_start.reshape(group_len, 1))

    got_rows, probs = lax.optimization_barrier((got_rows, probs))
    step_rows = SOURCES * caps
    steps = rows // step_rows
    flat_tiles = pl.BlockSpec((step_rows * 16, LANES), lambda i: (i, 0))
    wide = pl.BlockSpec((step_rows, width), lambda i: (i, 0))
    narrow = pl.BlockSpec((step_rows, ff), lambda i: (i, 0))
    w_in = whole((1, width, ff))
    w_out = whole((1, ff, width))
    narrow_shape = jax.ShapeDtypeStruct((rows, ff), BF16)
    wide_shape = jax.ShapeDtypeStruct((rows, width), BF16)
    rows_in, act, act_da, act_db = call(
        expert_up_kernel,
        (wide_shape, narrow_shape, narrow_shape, narrow_shape),
        flops=4 * rows * width * ff,
        moved=18000000,
        grid=(steps,),
        in_specs=[flat_tiles, whole((256, 256)), w_in, w_in],
        out_specs=(wide, narrow, narrow, narrow),
    )(got_rows, swap, w_gate, w_up)
    index = np.arange(step_rows)
    gather = jnp.asarray(index[None, :] // caps == np.arange(SOURCES)[:, None], BF16)
    spread = jnp.asarray(index[:, None] % caps == np.arange(LANES)[None, :], BF16)
    block_rows = caps * 16 + PACK_EXTRA
    scaled_grad, pre_grad, up_grad, send_back = call(
        functools.partial(expert_down_kernel, caps),
        (
            wide_shape,
            narrow_shape,
            narrow_shape,
            jax.ShapeDtypeStruct((experts, block_rows, LANES), BF16),
        ),
        flops=6 * rows * width * ff,
        moved=25000000,
        grid=(steps,),
        in_specs=[
            flat_tiles,
            whole((256, 256)),
            whole((SOURCES, step_rows)),
            whole((step_rows, LANES)),
            w_in,
            w_in,
            w_out,
            narrow,
            narrow,
            narrow,
        ],
        out_specs=(
            wide,
            narrow,
            narrow,
            pl.BlockSpec((SOURCES, block_rows, LANES), lambda i: (i, 0, 0)),
        ),
        scratch_shapes=[pltpu.VMEM((step_rows, width), BF16)],
    )(got_grads, swap, gather, spread, w_gate, w_up, w_down, act, act_da, act_db)
    back = exchange(send_back)
    grad_scale = (tokens * top_k) ** (-0.5)

    def weight_grad(left, right):
        product = lax.dot_general(left, right, FIRST, preferred_element_type=F32)
        return (product * grad_scale).astype(BF16)[None]

    grad_gate_w = weight_grad(rows_in, pre_grad)
    grad_up_w = weight_grad(rows_in, up_grad)
    grad_down_w = weight_grad(act, scaled_grad)

    back, grad_gate_w, grad_up_w, grad_down_w = lax.optimization_barrier(
        (back, grad_gate_w, grad_up_w, grad_down_w)
    )
    residual_grad = call(
        combine_kernel,
        jax.ShapeDtypeStruct((tokens, width), BF16),
        moved=8000000,
        grid_spec=pltpu.PrefetchScalarGridSpec(
            num_scalar_prefetch=2,
            grid=(1,),
            in_specs=[
                whole(back.shape),
                whole((tokens, CHUNKS, LANES)),
                whole((tokens, CHUNKS, LANES)),
                whole((CHUNKS, LANES)),
                whole((256, 256)),
            ],
            out_specs=whole((tokens, width)),
            scratch_shapes=[
                pltpu.VMEM((tokens, CHUNKS, LANES), F32),
                pltpu.VMEM((tokens * CHUNKS, LANES), BF16),
            ],
        ),
    )(ids_t, slots, back, hidden3, grad3, gain2, swap)
    gate_grad = call(gate_kernel, jax.ShapeDtypeStruct((top_k, tokens), BF16), moved=200000)(
        ids_t, slots, weight_t, back[:, caps * 16, :]
    ).T

    group_rows = lax.all_gather(residual_grad, "ep", axis=0, tiled=True)
    group_rows, gate_grad = lax.optimization_barrier((group_rows, gate_grad))
    partial_w = lax.dot_general(
        group_rows, attn_out, FIRST, preferred_element_type=F32
    ).astype(BF16)
    pieces = lax.all_to_all(
        partial_w.reshape(dp_size, width // dp_size, head_cols),
        "dp",
        split_axis=0,
        concat_axis=0,
        tiled=True,
    )
    out_weight_grad = (
        jnp.sum(pieces.astype(F32), axis=0) * (group_len * dp_size) ** (-0.5)
    ).astype(BF16)
    attn_grad = jnp.dot(group_rows, out_weight, preferred_element_type=F32).astype(BF16)
    head_shape = jax.ShapeDtypeStruct((group_len, head_cols), BF16)
    query_grad, key_grad, value_grad = call(
        attention_kernel,
        (head_shape, head_shape, head_shape),
        flops=4 * 8 * SEQ * SEQ * HEAD_DIM,
        moved=6000000,
        grid=(seq_count, head_count),
        in_specs=[probs_block] + [head_block] * 5,
        out_specs=(head_block, head_block, head_block),
    )(probs, queries, keys, values, attn_out, attn_grad)
    return (
        gate_grad,
        grad_gate_w,
        grad_up_w,
        grad_down_w,
        residual_grad,
        out_weight_grad,
        query_grad,
        key_grad,
        value_grad,
    )


def solution(mesh):
    tokens = P(("dp", "ep"), None)
    expert = P(("ep", "dp"), None, None)
    heads = P("dp", "ep")
    return jax.shard_map(
        per_device,
        mesh=mesh,
        in_specs=(
            tokens,
            tokens,
            P(),
            tokens,
            tokens,
            expert,
            expert,
            expert,
            heads,
            heads,
            heads,
            heads,
            P(None, "ep"),
            P("dp"),
        ),
        out_specs=(tokens, expert, expert, expert, tokens, heads, heads, heads, heads),
        check_vma=False,
    )
```

```python
import functools

import jax
import jax.numpy as jnp
import numpy as np
from jax import lax
from jax.experimental import pallas as pl
from jax.experimental.pallas import tpu as pltpu
from jax.sharding import PartitionSpec as P

HEAD_DIM = 128
SEQ = 512
EPS = 1e-06
LANES = 128
CHUNKS = 16
F32 = jnp.float32
BF16 = jnp.bfloat16
MESH = pl.DeviceIdType.MESH
LAST = (((1,), (1,)), ((), ()))
FIRST = (((0,), (0,)), ((), ()))
PACK_EXTRA = 8
DESTS = 32
SOURCES = 32
VMEM_LIMIT = 56 * 1024 * 1024


def swap_matrix():
    index = np.arange(256)
    matrix = np.zeros((256, 256), np.float32)
    matrix[(index % 16) * 16 + index // 16, index] = 1.0
    return jnp.asarray(matrix, BF16)


def call(kernel, out_shape, flops=0, moved=0, **kwargs):
    return pl.pallas_call(
        kernel,
        out_shape=out_shape,
        compiler_params=pltpu.CompilerParams(vmem_limit_bytes=VMEM_LIMIT),
        cost_estimate=pl.CostEstimate(flops=flops, bytes_accessed=moved, transcendentals=0),
        **kwargs,
    )


def whole(shape):
    return pl.BlockSpec(shape, lambda *_: (0,) * len(shape))


def tiles_to_rows(get_tiles, swap, out_ref, groups):
    for group in range(groups):
        pair = jnp.concatenate([get_tiles(2 * group), get_tiles(2 * group + 1)], axis=1)
        turned = jnp.dot(swap, pair, preferred_element_type=F32).astype(BF16)
        for chunk in range(CHUNKS):
            cols = slice(chunk * LANES, (chunk + 1) * LANES)
            rows = turned[chunk * 16 : (chunk + 1) * 16]
            out_ref[group * 32 : group * 32 + 16, cols] = rows[:, :LANES]
            out_ref[group * 32 + 16 : group * 32 + 32, cols] = rows[:, LANES:]


def slots_kernel(caps, ids_ref, weight_ref, table_ref, scale_ref, slot_ref):
    top_k, tokens = ids_ref.shape
    experts = LANES
    lane = lax.broadcasted_iota(jnp.int32, (experts, tokens), 1)
    row = lax.broadcasted_iota(jnp.int32, (experts, tokens), 0)
    ids = ids_ref[...]
    weight = weight_ref[...].astype(F32)
    chosen = jnp.zeros((experts, tokens), F32)
    weights = jnp.zeros((experts, tokens), F32)
    for k in range(top_k):
        hit = ids[k : k + 1] == row
        chosen = jnp.where(hit, 1.0, chosen)
        weights = jnp.where(hit, weight[k : k + 1], weights)
    upper = jnp.where(row < lane, 1.0, 0.0).astype(BF16)
    counts = jnp.dot(chosen.astype(BF16), upper, preferred_element_type=F32)
    table = jnp.zeros((experts, LANES), F32)
    scales = jnp.zeros((experts, LANES), F32)
    from_end = (lane - tokens).astype(F32)
    for place in range(caps):
        mask = (chosen > 0.5) & (jnp.abs(counts - place) < 0.5)
        token = jnp.sum(jnp.where(mask, from_end, 0.0), axis=1, keepdims=True) + tokens
        scale = jnp.sum(jnp.where(mask, weights, 0.0), axis=1, keepdims=True)
        table = jnp.where(lane == place, token, table)
        scales = jnp.where(lane == place, scale, scales)
    table_ref[...] = table.astype(jnp.int32)
    scale_ref[...] = scales
    slot_ref[...] = jnp.concatenate(
        [
            jnp.sum(jnp.where(ids[k : k + 1] == row, counts, 0.0), axis=0, keepdims=True)
            for k in range(top_k)
        ],
        axis=0,
    ).astype(jnp.int32)


def pack_rows_kernel(table_ref, hidden_ref, gain_ref, out_ref, normed):
    tokens = hidden_ref.shape[0]
    step = pl.program_id(0)
    caps = out_ref.shape[0] // DESTS

    @pl.when(step == 0)
    def _():
        gain = gain_ref[...].astype(F32)[None]
        for start in range(0, tokens, 16):
            hidden = hidden_ref[start : start + 16].astype(F32)
            mean = jnp.sum(
                jnp.sum(hidden * hidden, axis=2, keepdims=True), axis=1, keepdims=True
            ) * (1.0 / (CHUNKS * LANES))
            normed[start : start + 16] = (hidden * lax.rsqrt(mean + EPS) * gain).astype(BF16)
        normed[tokens] = jnp.zeros((CHUNKS, LANES), BF16)

    def fill(dest, carry):
        for place in range(caps):
            out_ref[dest * caps + place] = normed[table_ref[step * DESTS + dest, place]]
        return carry

    lax.fori_loop(0, DESTS, fill, 0, unroll=2)


def pack_grads_kernel(table_ref, scale_ref, grad_ref, out_ref):
    tokens = grad_ref.shape[0]
    step = pl.program_id(0)
    caps = out_ref.shape[0] // DESTS

    def fill(dest, carry):
        for place in range(caps):
            at = step * DESTS + dest
            token = jnp.minimum(table_ref[at, place], tokens - 1)
            scale = scale_ref[at, place]
            out_ref[dest * caps + place] = (grad_ref[token].astype(F32) * scale).astype(BF16)
        return carry

    lax.fori_loop(0, DESTS, fill, 0, unroll=2)


def expert_up_kernel(tile_ref, swap_ref, gate_w_ref, up_w_ref, row_ref, act_ref, da_ref, db_ref):
    rows = row_ref.shape[0]
    tiles_to_rows(
        lambda i: tile_ref[i * 256 : (i + 1) * 256], swap_ref[...], row_ref, rows // 32
    )
    gate = jnp.dot(row_ref[...], gate_w_ref[0], preferred_element_type=F32)
    up = jnp.dot(row_ref[...], up_w_ref[0], preferred_element_type=F32)
    sig = 1.0 / (1.0 + jnp.exp(-gate))
    silu = gate * sig
    act_ref[...] = (silu * up).astype(BF16)
    da_ref[...] = (up * sig * (1.0 + gate * (1.0 - sig))).astype(BF16)
    db_ref[...] = silu.astype(BF16)


def expert_down_kernel(
    caps,
    tile_ref,
    swap_ref,
    gather_ref,
    spread_ref,
    gate_w_ref,
    up_w_ref,
    down_w_ref,
    act_ref,
    da_ref,
    db_ref,
    grad_ref,
    pre_ref,
    upg_ref,
    back_ref,
    rowg,
):
    rows = grad_ref.shape[0]
    swap = swap_ref[...]
    tiles_to_rows(lambda i: tile_ref[i * 256 : (i + 1) * 256], swap, grad_ref, rows // 32)
    act_grad = lax.dot_general(grad_ref[...], down_w_ref[0], LAST, preferred_element_type=F32)
    pre = (act_grad * da_ref[...].astype(F32)).astype(BF16)
    upg = (act_grad * db_ref[...].astype(F32)).astype(BF16)
    pre_ref[...] = pre
    upg_ref[...] = upg
    score = jnp.sum(act_grad * act_ref[...].astype(F32), axis=1, keepdims=True)
    placed = jnp.dot(
        gather_ref[...],
        (score * spread_ref[...].astype(F32)).astype(BF16),
        preferred_element_type=F32,
    ).astype(BF16)
    rowg[...] = (
        lax.dot_general(pre, gate_w_ref[0], LAST, preferred_element_type=F32)
        + lax.dot_general(upg, up_w_ref[0], LAST, preferred_element_type=F32)
    ).astype(BF16)
    for group in range(rows // 32):
        halves = []
        for side in range(2):
            at = group * 32 + side * 16
            halves.append(
                jnp.concatenate(
                    [
                        rowg[at : at + 16, chunk * LANES : (chunk + 1) * LANES]
                        for chunk in range(CHUNKS)
                    ],
                    axis=0,
                )
            )
        turned = jnp.dot(
            swap, jnp.concatenate(halves, axis=1), preferred_element_type=F32
        ).astype(BF16)
        for side in range(2):
            for inner in range(16):
                row = group * 32 + side * 16 + inner
                place = (row % caps) * 16
                back_ref[row // caps, place : place + 16, :] = turned[
                    inner * 16 : (inner + 1) * 16, side * LANES : (side + 1) * LANES
                ]
    for source in range(rows // caps):
        back_ref[source, caps * 16 : caps * 16 + PACK_EXTRA, :] = jnp.broadcast_to(
            placed[source : source + 1], (PACK_EXTRA, LANES)
        )


def combine_kernel(
    ids_ref,
    slot_ref,
    back_ref,
    hidden_ref,
    grad_ref,
    gain_ref,
    swap_ref,
    id_lanes,
    slot_lanes,
    weight_ref,
    out_ref,
    gate_ref,
    total,
    tiles,
):
    top_k, tokens = ids_ref.shape

    def gather(token, carry):
        acc = jnp.zeros((CHUNKS, LANES), F32)
        for k in range(top_k):
            at = pl.multiple_of(slot_ref[k, token] * 16, 16)
            acc = acc + back_ref[ids_ref[k, token], pl.ds(at, 16), :].astype(F32)
        total[token] = acc
        return carry

    lax.fori_loop(0, tokens, gather, 0, unroll=4)
    gain = gain_ref[...].astype(F32)[None]
    share = 1.0 / (CHUNKS * LANES)

    def mean(value):
        return (
            jnp.sum(jnp.sum(value, axis=2, keepdims=True), axis=1, keepdims=True) * share
        )

    for start in range(0, tokens, 16):
        hidden = hidden_ref[start : start + 16].astype(F32)
        inv_rms = lax.rsqrt(mean(hidden * hidden) + EPS)
        unit = hidden * inv_rms
        scaled = total[start : start + 16] * gain
        residual = grad_ref[start : start + 16].astype(F32) + inv_rms * (
            scaled - unit * mean(scaled * unit)
        )
        tiles[start * 16 : start * 16 + 256] = residual.astype(BF16).reshape(256, LANES)
    tiles_to_rows(
        lambda i: tiles[i * 256 : (i + 1) * 256], swap_ref[...], out_ref, tokens // 32
    )
    extra = back_ref[:, back_ref.shape[1] - PACK_EXTRA :, :].astype(F32)
    score = (jnp.sum(extra, axis=1) * (1.0 / PACK_EXTRA)).astype(BF16)
    write_gate(id_lanes[...], slot_lanes[...], weight_ref[...], score, gate_ref)


def write_gate(ids, slot, weight, score, out_ref):
    top_k, tokens = ids.shape
    row = lax.broadcasted_iota(jnp.int32, (LANES, tokens), 0)
    found = []
    for k in range(top_k):
        hit = jnp.where(ids[k : k + 1] == row, 1.0, 0.0).astype(BF16)
        mine = lax.dot_general(score, hit, FIRST, preferred_element_type=F32)
        found.append(
            jnp.sum(jnp.where(slot[k : k + 1] == row, mine, 0.0), axis=0, keepdims=True)
        )
    scale = (CHUNKS * LANES) ** (-0.5)
    value = jnp.concatenate(found, axis=0) * scale / weight.astype(F32)
    out_ref[...] = value.astype(BF16)


def probs_kernel(query_ref, key_ref, begin_ref, out_ref):
    scores = lax.dot_general(
        query_ref[...], key_ref[...], LAST, preferred_element_type=F32
    ) * HEAD_DIM ** (-0.5)
    here = lax.broadcasted_iota(jnp.int32, (SEQ, SEQ), 0)
    there = lax.broadcasted_iota(jnp.int32, (SEQ, SEQ), 1)
    visible = (there <= here) & (there >= begin_ref[...])
    masked = jnp.where(visible, scores, -1e30)
    top = jnp.max(masked, axis=1, keepdims=True)
    weights = jnp.where(visible, jnp.exp(masked - top), 0.0)
    out_ref[0, 0] = (weights / jnp.sum(weights, axis=1, keepdims=True)).astype(BF16)


def tail_kernel(
    sum_scale,
    resid_hbm,
    weight_hbm,
    attn_hbm,
    probs_hbm,
    query_hbm,
    key_hbm,
    value_hbm,
    dq_ref,
    dk_ref,
    dv_ref,
    out_ref,
    group,
    weight,
    attn,
    probs,
    query,
    key,
    value,
    grads,
    acc,
    pieces,
    arrived,
    load_sems,
    ring_send,
    ring_recv,
    side_send,
    side_recv,
    dp_send,
    dp_recv,
):
    ep, dp = lax.axis_index("ep"), lax.axis_index("dp")
    chips = lax.axis_size("ep") // 2
    dp_size = lax.axis_size("dp")
    chip, core = ep // 2, ep % 2
    tokens, width = resid_hbm.shape
    half = tokens // 2
    above = ((chip + 1) % chips) * 2 + core
    below = ((chip + chips - 1) % chips) * 2 + core
    across = ((chip + 2) % chips) * 2 + core
    sibling = chip * 2 + 1 - core

    barrier = pltpu.get_barrier_semaphore()
    for peer in (above, below, sibling):
        pl.semaphore_signal(barrier, inc=1, device_id=(peer, dp), device_id_type=MESH)
    for step in range(1, dp_size):
        pl.semaphore_signal(
            barrier, inc=1, device_id=(ep, (dp + step) % dp_size), device_id_type=MESH
        )

    loads = [
        pltpu.make_async_copy(source, target, load_sems.at[number])
        for number, (source, target) in enumerate(
            (
                (resid_hbm, group.at[pl.ds(pl.multiple_of(ep * tokens, tokens), tokens)]),
                (weight_hbm, weight),
                (attn_hbm, attn),
                (query_hbm, query),
                (key_hbm, key),
                (value_hbm, value),
                (probs_hbm, probs),
            )
        )
    ]
    for load in loads:
        load.start()
    loads[0].wait()
    pl.semaphore_wait(barrier, dp_size - 1 + 3)

    def part(owner, second):
        at = pl.multiple_of(owner * tokens + second * half, half)
        return group.at[pl.ds(at, half)]

    def ring(number, owner, second, target):
        return pltpu.make_async_remote_copy(
            src_ref=part(owner, second),
            dst_ref=part(owner, second),
            send_sem=ring_send.at[number],
            recv_sem=ring_recv.at[number],
            device_id=(target, dp),
            device_id_type=MESH,
        )

    def side(number, owner, second):
        return pltpu.make_async_remote_copy(
            src_ref=part(owner, second),
            dst_ref=part(owner, second),
            send_sem=side_send.at[number],
            recv_sem=side_recv.at[number],
            device_id=(sibling, dp),
            device_id_type=MESH,
        )

    up = [ring(0, ep, 0, above), ring(1, ep, 1, above)]
    down = [ring(3, ep, 0, below), ring(2, ep, 1, below)]
    own = [side(0, ep, 0), side(1, ep, 1)]
    for copy in (up[0], down[1], own[0], own[1], up[1], down[0]):
        copy.start()

    def matmuls(pair, last):
        at = pl.multiple_of(pair * 2 * tokens, 2 * tokens)
        mine = pl.ds(at, 2 * tokens)
        grads[mine] = jnp.dot(group[mine], weight[...], preferred_element_type=F32).astype(BF16)

        def add(step, carry):
            dest = (dp + 1 + step) % dp_size
            columns = pl.ds(pl.multiple_of(dest * tokens, tokens), tokens)
            product = lax.dot_general(
                group[mine, columns], attn[mine], FIRST, preferred_element_type=F32
            )
            if last is None:
                acc[dest] = product
            elif not last:
                acc[dest] = acc[dest] + product
            else:
                pieces[dest] = (acc[dest] + product).astype(BF16)
            return carry

        if not last:
            lax.fori_loop(0, dp_size, add, 0)
        else:
            for step in range(dp_size):
                add(step, 0)
                if step < dp_size - 1:
                    send_piece(step).start()

    def send_piece(step):
        dest = (dp + 1 + step) % dp_size
        return pltpu.make_async_remote_copy(
            src_ref=pieces.at[dest],
            dst_ref=arrived.at[dp],
            send_sem=dp_send.at[step],
            recv_sem=dp_recv.at[step],
            device_id=(ep, dest),
            device_id_type=MESH,
        )

    own[0].wait_recv()
    own[1].wait_recv()
    loads[1].wait()
    loads[2].wait()
    matmuls(chip, None)

    up[0].wait_recv()
    forward_up = ring(4, below, 0, above)
    forward_up.start()
    relay = [side(2, below, 0)]
    relay[0].start()
    down[1].wait_recv()
    forward_down = ring(5, above, 1, below)
    forward_down.start()
    relay.append(side(3, above, 1))
    relay[1].start()
    up[1].wait_recv()
    relay.append(side(4, below, 1))
    relay[2].start()
    down[0].wait_recv()
    relay.append(side(5, above, 0))
    relay[3].start()
    for copy in relay:
        copy.wait_recv()
    matmuls(below // 2, False)
    matmuls(above // 2, False)
    forward_up.wait_recv()
    relay.append(side(6, across, 0))
    relay[4].start()
    forward_down.wait_recv()
    relay.append(side(7, across, 1))
    relay[5].start()
    relay[4].wait_recv()
    relay[5].wait_recv()
    matmuls(across // 2, True)

    for load in loads[3:]:
        load.wait()
    heads = query.shape[1] // HEAD_DIM
    scale = HEAD_DIM ** (-0.5)

    def attend(number, carry):
        seq, head = number // heads, number % heads
        at = (
            pl.ds(pl.multiple_of(seq * SEQ, SEQ), SEQ),
            pl.ds(pl.multiple_of(head * HEAD_DIM, HEAD_DIM), HEAD_DIM),
        )
        grad = grads[at]
        weights = probs[number]
        delta = jnp.sum(grad.astype(F32) * attn[at].astype(F32), axis=1, keepdims=True)
        prob_grad = lax.dot_general(grad, value[at], LAST, preferred_element_type=F32)
        score_grad = (weights.astype(F32) * (prob_grad - delta)).astype(BF16)
        dq_ref[at] = (
            jnp.dot(score_grad, key[at], preferred_element_type=F32) * scale
        ).astype(BF16)
        dk_ref[at] = (
            lax.dot_general(score_grad, query[at], FIRST, preferred_element_type=F32) * scale
        ).astype(BF16)
        dv_ref[at] = lax.dot_general(weights, grad, FIRST, preferred_element_type=F32).astype(BF16)
        return carry

    lax.fori_loop(0, probs.shape[0], attend, 0)

    for step in range(dp_size - 1):
        send_piece(step).wait_recv()
    total = pieces[dp].astype(F32)
    for step in range(1, dp_size):
        total = total + arrived[(dp + step) % dp_size].astype(F32)
    out_ref[...] = (total * sum_scale).astype(BF16)
    for copy in up + down + own + relay + [forward_up, forward_down]:
        copy.wait_send()
    for step in range(dp_size - 1):
        send_piece(step).wait_send()


def per_device(
    hidden_state,
    out_grad,
    norm_gain,
    expert_ids,
    route_weight,
    w_gate,
    w_up,
    w_down,
    queries,
    keys,
    values,
    attn_out,
    out_weight,
    doc_start,
):
    tokens, width = hidden_state.shape
    top_k = expert_ids.shape[1]
    ff = w_gate.shape[2]
    dp_size = lax.axis_size("dp")
    experts = lax.axis_size("ep") * dp_size
    caps = 5 * tokens * top_k // (4 * experts)
    rows = experts * caps
    both = ("ep", "dp")
    swap = swap_matrix()
    hidden3 = hidden_state.reshape(tokens, CHUNKS, LANES)
    grad3 = out_grad.reshape(tokens, CHUNKS, LANES)
    gain2 = norm_gain.reshape(CHUNKS, LANES)

    ids_t, weight_t = expert_ids.T, route_weight.T
    table, scales, slots = call(
        functools.partial(slots_kernel, caps),
        (
            jax.ShapeDtypeStruct((experts, LANES), jnp.int32),
            jax.ShapeDtypeStruct((experts, LANES), F32),
            jax.ShapeDtypeStruct((top_k, tokens), jnp.int32),
        ),
        moved=300000,
    )(ids_t, weight_t)

    pack_block = pl.BlockSpec((DESTS * caps, CHUNKS, LANES), lambda i, *_: (i, 0, 0))

    def exchange(array):
        return lax.all_to_all(array, both, split_axis=0, concat_axis=0, tiled=True)

    def send(kernel, scalars, arrays, scratch):
        packed = call(
            kernel,
            jax.ShapeDtypeStruct((rows, CHUNKS, LANES), BF16),
            moved=6000000,
            grid_spec=pltpu.PrefetchScalarGridSpec(
                num_scalar_prefetch=len(scalars),
                grid=(experts // DESTS,),
                in_specs=[whole(a.shape) for a in arrays],
                out_specs=pack_block,
                scratch_shapes=scratch,
            ),
        )(*scalars, *arrays)
        return exchange(packed.reshape(experts, caps * 16, LANES)).reshape(rows * 16, LANES)

    table_scratch = [pltpu.VMEM((tokens + 1, CHUNKS, LANES), BF16)]
    got_rows = send(pack_rows_kernel, [table], [hidden3, gain2], table_scratch)
    got_grads = send(pack_grads_kernel, [table, scales], [grad3], [])

    group_len, head_cols = queries.shape
    head_count = head_cols // HEAD_DIM
    seq_count = group_len // SEQ
    head_block = pl.BlockSpec((SEQ, HEAD_DIM), lambda s, h: (s, h))
    probs_block = pl.BlockSpec((1, 1, SEQ, SEQ), lambda s, h: (s, h, 0, 0))
    probs = call(
        probs_kernel,
        jax.ShapeDtypeStruct((seq_count, head_count, SEQ, SEQ), BF16),
        flops=10**10,
        moved=5000000,
        grid=(seq_count, head_count),
        in_specs=[head_block, head_block, pl.BlockSpec((SEQ, 1), lambda s, h: (s, 0))],
        out_specs=probs_block,
    )(queries, keys, doc_start.reshape(group_len, 1))

    got_rows, probs = lax.optimization_barrier((got_rows, probs))
    step_rows = SOURCES * caps
    steps = rows // step_rows
    flat_tiles = pl.BlockSpec((step_rows * 16, LANES), lambda i: (i, 0))
    wide = pl.BlockSpec((step_rows, width), lambda i: (i, 0))
    narrow = pl.BlockSpec((step_rows, ff), lambda i: (i, 0))
    w_in = whole((1, width, ff))
    w_out = whole((1, ff, width))
    narrow_shape = jax.ShapeDtypeStruct((rows, ff), BF16)
    wide_shape = jax.ShapeDtypeStruct((rows, width), BF16)
    rows_in, act, act_da, act_db = call(
        expert_up_kernel,
        (wide_shape, narrow_shape, narrow_shape, narrow_shape),
        flops=4 * rows * width * ff,
        moved=18000000,
        grid=(steps,),
        in_specs=[flat_tiles, whole((256, 256)), w_in, w_in],
        out_specs=(wide, narrow, narrow, narrow),
    )(got_rows, swap, w_gate, w_up)
    index = np.arange(step_rows)
    gather = jnp.asarray(index[None, :] // caps == np.arange(SOURCES)[:, None], BF16)
    spread = jnp.asarray(index[:, None] % caps == np.arange(LANES)[None, :], BF16)
    block_rows = caps * 16 + PACK_EXTRA
    scaled_grad, pre_grad, up_grad, send_back = call(
        functools.partial(expert_down_kernel, caps),
        (
            wide_shape,
            narrow_shape,
            narrow_shape,
            jax.ShapeDtypeStruct((experts, block_rows, LANES), BF16),
        ),
        flops=6 * rows * width * ff,
        moved=25000000,
        grid=(steps,),
        in_specs=[
            flat_tiles,
            whole((256, 256)),
            whole((SOURCES, step_rows)),
            whole((step_rows, LANES)),
            w_in,
            w_in,
            w_out,
            narrow,
            narrow,
            narrow,
        ],
        out_specs=(
            wide,
            narrow,
            narrow,
            pl.BlockSpec((SOURCES, block_rows, LANES), lambda i: (i, 0, 0)),
        ),
        scratch_shapes=[pltpu.VMEM((step_rows, width), BF16)],
    )(got_grads, swap, gather, spread, w_gate, w_up, w_down, act, act_da, act_db)
    back = exchange(send_back)
    grad_scale = (tokens * top_k) ** (-0.5)

    def weight_grad(left, right):
        product = lax.dot_general(left, right, FIRST, preferred_element_type=F32)
        return (product * grad_scale).astype(BF16)[None]

    grad_gate_w = weight_grad(rows_in, pre_grad)
    grad_up_w = weight_grad(rows_in, up_grad)
    grad_down_w = weight_grad(act, scaled_grad)

    back, grad_gate_w, grad_up_w, grad_down_w = lax.optimization_barrier(
        (back, grad_gate_w, grad_up_w, grad_down_w)
    )
    residual_grad, gate_grad = call(
        combine_kernel,
        (
            jax.ShapeDtypeStruct((tokens, width), BF16),
            jax.ShapeDtypeStruct((top_k, tokens), BF16),
        ),
        moved=8000000,
        grid_spec=pltpu.PrefetchScalarGridSpec(
            num_scalar_prefetch=2,
            grid=(1,),
            in_specs=[
                whole(back.shape),
                whole((tokens, CHUNKS, LANES)),
                whole((tokens, CHUNKS, LANES)),
                whole((CHUNKS, LANES)),
                whole((256, 256)),
                whole((top_k, tokens)),
                whole((top_k, tokens)),
                whole((top_k, tokens)),
            ],
            out_specs=(whole((tokens, width)), whole((top_k, tokens))),
            scratch_shapes=[
                pltpu.VMEM((tokens, CHUNKS, LANES), F32),
                pltpu.VMEM((tokens * CHUNKS, LANES), BF16),
            ],
        ),
    )(ids_t, slots, back, hidden3, grad3, gain2, swap, ids_t, slots, weight_t)
    gate_grad = gate_grad.T

    any_spec = pl.BlockSpec(memory_space=pl.ANY)
    vmem_spec = pl.BlockSpec(memory_space=pltpu.VMEM)
    head_shape = jax.ShapeDtypeStruct((group_len, head_cols), BF16)
    head_vmem = pltpu.VMEM((group_len, head_cols), BF16)
    piece_shape = (dp_size, width // dp_size, head_cols)
    query_grad, key_grad, value_grad, out_weight_grad = pl.pallas_call(
        functools.partial(tail_kernel, (group_len * dp_size) ** (-0.5)),
        out_shape=(
            head_shape,
            head_shape,
            head_shape,
            jax.ShapeDtypeStruct(piece_shape[1:], BF16),
        ),
        in_specs=[any_spec] * 7,
        out_specs=(vmem_spec,) * 4,
        scratch_shapes=[
            pltpu.VMEM((group_len, width), BF16),
            pltpu.VMEM((width, head_cols), BF16),
            head_vmem,
            pltpu.VMEM((seq_count * head_count, SEQ, SEQ), BF16),
            head_vmem,
            head_vmem,
            head_vmem,
            head_vmem,
            pltpu.VMEM(piece_shape, F32),
            pltpu.VMEM(piece_shape, BF16),
            pltpu.VMEM(piece_shape, BF16),
            pltpu.SemaphoreType.DMA((7,)),
            pltpu.SemaphoreType.DMA((6,)),
            pltpu.SemaphoreType.DMA((6,)),
            pltpu.SemaphoreType.DMA((8,)),
            pltpu.SemaphoreType.DMA((8,)),
            pltpu.SemaphoreType.DMA((dp_size - 1,)),
            pltpu.SemaphoreType.DMA((dp_size - 1,)),
        ],
        compiler_params=pltpu.CompilerParams(
            collective_id=0, has_side_effects=True, vmem_limit_bytes=VMEM_LIMIT
        ),
        cost_estimate=pl.CostEstimate(
            flops=4 * 10**9, bytes_accessed=20000000, transcendentals=0
        ),
    )(
        residual_grad,
        out_weight,
        attn_out,
        probs.reshape(seq_count * head_count, SEQ, SEQ),
        queries,
        keys,
        values,
    )
    return (
        gate_grad,
        grad_gate_w,
        grad_up_w,
        grad_down_w,
        residual_grad,
        out_weight_grad,
        query_grad,
        key_grad,
        value_grad,
    )


def solution(mesh):
    tokens = P(("dp", "ep"), None)
    expert = P(("ep", "dp"), None, None)
    heads = P("dp", "ep")
    return jax.shard_map(
        per_device,
        mesh=mesh,
        in_specs=(
            tokens,
            tokens,
            P(),
            tokens,
            tokens,
            expert,
            expert,
            expert,
            heads,
            heads,
            heads,
            heads,
            P(None, "ep"),
            P("dp"),
        ),
        out_specs=(tokens, expert, expert, expert, tokens, heads, heads, heads, heads),
        check_vma=False,
    )
```

```python
import functools

import jax
import jax.numpy as jnp
import numpy as np
from jax import lax
from jax.experimental import pallas as pl
from jax.experimental.pallas import tpu as pltpu
from jax.sharding import PartitionSpec as P

HEAD_DIM = 128
SEQ = 512
EPS = 1e-06
LANES = 128
CHUNKS = 16
F32 = jnp.float32
BF16 = jnp.bfloat16
MESH = pl.DeviceIdType.MESH
LAST = (((1,), (1,)), ((), ()))
FIRST = (((0,), (0,)), ((), ()))
PACK_EXTRA = 8
DESTS = 32
SOURCES = 32
VMEM_LIMIT = 56 * 1024 * 1024


def swap_matrix():
    index = np.arange(256)
    matrix = np.zeros((256, 256), np.float32)
    matrix[(index % 16) * 16 + index // 16, index] = 1.0
    return jnp.asarray(matrix, BF16)


def call(kernel, out_shape, flops=0, moved=0, **kwargs):
    return pl.pallas_call(
        kernel,
        out_shape=out_shape,
        compiler_params=pltpu.CompilerParams(vmem_limit_bytes=VMEM_LIMIT),
        cost_estimate=pl.CostEstimate(flops=flops, bytes_accessed=moved, transcendentals=0),
        **kwargs,
    )


def whole(shape):
    return pl.BlockSpec(shape, lambda *_: (0,) * len(shape))


def tiles_to_rows(get_tiles, swap, out_ref, groups):
    for group in range(groups):
        pair = jnp.concatenate([get_tiles(2 * group), get_tiles(2 * group + 1)], axis=1)
        turned = jnp.dot(swap, pair, preferred_element_type=F32).astype(BF16)
        for chunk in range(CHUNKS):
            cols = slice(chunk * LANES, (chunk + 1) * LANES)
            rows = turned[chunk * 16 : (chunk + 1) * 16]
            out_ref[group * 32 : group * 32 + 16, cols] = rows[:, :LANES]
            out_ref[group * 32 + 16 : group * 32 + 32, cols] = rows[:, LANES:]


def turn_rows(rows, swap):
    halves = [
        jnp.concatenate(
            [
                rows[side * 16 : side * 16 + 16, chunk * LANES : (chunk + 1) * LANES]
                for chunk in range(CHUNKS)
            ],
            axis=0,
        )
        for side in range(2)
    ]
    pair = jnp.concatenate(halves, axis=1)
    return jnp.dot(swap, pair, preferred_element_type=F32).astype(BF16)


def slots_kernel(caps, ids_ref, weight_ref, table_ref, scale_ref, slot_ref):
    top_k, tokens = ids_ref.shape
    experts = LANES
    lane = lax.broadcasted_iota(jnp.int32, (experts, tokens), 1)
    row = lax.broadcasted_iota(jnp.int32, (experts, tokens), 0)
    ids = ids_ref[...]
    weight = weight_ref[...].astype(F32)
    chosen = jnp.zeros((experts, tokens), F32)
    weights = jnp.zeros((experts, tokens), F32)
    for k in range(top_k):
        hit = ids[k : k + 1] == row
        chosen = jnp.where(hit, 1.0, chosen)
        weights = jnp.where(hit, weight[k : k + 1], weights)
    upper = jnp.where(row < lane, 1.0, 0.0).astype(BF16)
    counts = jnp.dot(chosen.astype(BF16), upper, preferred_element_type=F32)
    table = jnp.zeros((experts, LANES), F32)
    scales = jnp.zeros((experts, LANES), F32)
    from_end = (lane - tokens).astype(F32)
    for place in range(caps):
        mask = (chosen > 0.5) & (jnp.abs(counts - place) < 0.5)
        token = jnp.sum(jnp.where(mask, from_end, 0.0), axis=1, keepdims=True) + tokens
        scale = jnp.sum(jnp.where(mask, weights, 0.0), axis=1, keepdims=True)
        table = jnp.where(lane == place, token, table)
        scales = jnp.where(lane == place, scale, scales)
    table_ref[...] = table.T[:16].astype(jnp.int32)
    scale_ref[...] = scales.T[:16]
    slot_ref[...] = jnp.concatenate(
        [
            jnp.sum(jnp.where(ids[k : k + 1] == row, counts, 0.0), axis=0, keepdims=True)
            for k in range(top_k)
        ],
        axis=0,
    ).astype(jnp.int32)


def pack_rows_kernel(table_ref, hidden_ref, gain_ref, swap_ref, out_ref, normed):
    tokens, width = hidden_ref.shape
    step = pl.program_id(0)
    caps = out_ref.shape[0] // DESTS

    @pl.when(step == 0)
    def _():
        gain = gain_ref[...].astype(F32)
        swap = swap_ref[...]
        for start in range(0, tokens, 32):
            hidden = hidden_ref[start : start + 32].astype(F32)
            mean = jnp.sum(hidden * hidden, axis=1, keepdims=True) * (1.0 / width)
            low = (hidden * lax.rsqrt(mean + EPS) * gain).astype(BF16)
            turned = turn_rows(low, swap)
            for side in range(2):
                for inner in range(16):
                    normed[start + side * 16 + inner] = turned[
                        inner * 16 : (inner + 1) * 16, side * LANES : (side + 1) * LANES
                    ]
        normed[tokens] = jnp.zeros((CHUNKS, LANES), BF16)

    def fill(dest, carry):
        for place in range(caps):
            out_ref[dest * caps + place] = normed[table_ref[place, step * DESTS + dest]]
        return carry

    lax.fori_loop(0, DESTS, fill, 0, unroll=2)


def pack_grads_kernel(table_ref, scale_ref, grad_ref, out_ref):
    tokens = grad_ref.shape[0]
    step = pl.program_id(0)
    caps = out_ref.shape[0] // DESTS

    def fill(dest, carry):
        for place in range(caps):
            at = step * DESTS + dest
            token = jnp.minimum(table_ref[place, at], tokens - 1)
            scale = scale_ref[place, at]
            out_ref[dest * caps + place] = (grad_ref[token].astype(F32) * scale).astype(BF16)
        return carry

    lax.fori_loop(0, DESTS, fill, 0, unroll=2)


def expert_up_kernel(tile_ref, swap_ref, gate_w_ref, up_w_ref, row_ref, act_ref, da_ref, db_ref):
    rows = row_ref.shape[0]
    tiles_to_rows(
        lambda i: tile_ref[i * 256 : (i + 1) * 256], swap_ref[...], row_ref, rows // 32
    )
    gate = jnp.dot(row_ref[...], gate_w_ref[0], preferred_element_type=F32)
    up = jnp.dot(row_ref[...], up_w_ref[0], preferred_element_type=F32)
    sig = 1.0 / (1.0 + jnp.exp(-gate))
    silu = gate * sig
    act_ref[...] = (silu * up).astype(BF16)
    da_ref[...] = (up * sig * (1.0 + gate * (1.0 - sig))).astype(BF16)
    db_ref[...] = silu.astype(BF16)


def expert_down_kernel(
    caps,
    tile_ref,
    swap_ref,
    gather_ref,
    spread_ref,
    gate_w_ref,
    up_w_ref,
    down_w_ref,
    act_ref,
    da_ref,
    db_ref,
    grad_ref,
    pre_ref,
    upg_ref,
    back_ref,
    rowg,
):
    rows = grad_ref.shape[0]
    swap = swap_ref[...]
    tiles_to_rows(lambda i: tile_ref[i * 256 : (i + 1) * 256], swap, grad_ref, rows // 32)
    act_grad = lax.dot_general(grad_ref[...], down_w_ref[0], LAST, preferred_element_type=F32)
    pre = (act_grad * da_ref[...].astype(F32)).astype(BF16)
    upg = (act_grad * db_ref[...].astype(F32)).astype(BF16)
    pre_ref[...] = pre
    upg_ref[...] = upg
    score = jnp.sum(act_grad * act_ref[...].astype(F32), axis=1, keepdims=True)
    placed = jnp.dot(
        gather_ref[...],
        (score * spread_ref[...].astype(F32)).astype(BF16),
        preferred_element_type=F32,
    ).astype(BF16)
    rowg[...] = (
        lax.dot_general(pre, gate_w_ref[0], LAST, preferred_element_type=F32)
        + lax.dot_general(upg, up_w_ref[0], LAST, preferred_element_type=F32)
    ).astype(BF16)
    for group in range(rows // 32):
        halves = []
        for side in range(2):
            at = group * 32 + side * 16
            halves.append(
                jnp.concatenate(
                    [
                        rowg[at : at + 16, chunk * LANES : (chunk + 1) * LANES]
                        for chunk in range(CHUNKS)
                    ],
                    axis=0,
                )
            )
        turned = jnp.dot(
            swap, jnp.concatenate(halves, axis=1), preferred_element_type=F32
        ).astype(BF16)
        for side in range(2):
            for inner in range(16):
                row = group * 32 + side * 16 + inner
                place = (row % caps) * 16
                back_ref[row // caps, place : place + 16, :] = turned[
                    inner * 16 : (inner + 1) * 16, side * LANES : (side + 1) * LANES
                ]
    for source in range(rows // caps):
        back_ref[source, caps * 16 : caps * 16 + PACK_EXTRA, :] = jnp.broadcast_to(
            placed[source : source + 1], (PACK_EXTRA, LANES)
        )


def combine_kernel(
    ids_ref,
    slot_ref,
    back_ref,
    hidden_ref,
    grad_ref,
    gain_ref,
    swap_ref,
    id_lanes,
    slot_lanes,
    weight_ref,
    out_ref,
    gate_ref,
    total,
    tiles,
):
    top_k, tokens = ids_ref.shape

    def gather(token, carry):
        acc = jnp.zeros((CHUNKS, LANES), F32)
        for k in range(top_k):
            at = pl.multiple_of(slot_ref[k, token] * 16, 16)
            acc = acc + back_ref[ids_ref[k, token], pl.ds(at, 16), :].astype(F32)
        total[token] = acc
        return carry

    lax.fori_loop(0, tokens, gather, 0, unroll=4)
    gain = gain_ref[...].astype(F32)[None]
    share = 1.0 / (CHUNKS * LANES)

    def mean(value):
        return (
            jnp.sum(jnp.sum(value, axis=2, keepdims=True), axis=1, keepdims=True) * share
        )

    for start in range(0, tokens, 16):
        hidden = hidden_ref[start : start + 16].astype(F32)
        inv_rms = lax.rsqrt(mean(hidden * hidden) + EPS)
        unit = hidden * inv_rms
        scaled = total[start : start + 16] * gain
        residual = grad_ref[start : start + 16].astype(F32) + inv_rms * (
            scaled - unit * mean(scaled * unit)
        )
        tiles[start * 16 : start * 16 + 256] = residual.astype(BF16).reshape(256, LANES)
    tiles_to_rows(
        lambda i: tiles[i * 256 : (i + 1) * 256], swap_ref[...], out_ref, tokens // 32
    )
    extra = back_ref[:, back_ref.shape[1] - PACK_EXTRA :, :].astype(F32)
    score = (jnp.sum(extra, axis=1) * (1.0 / PACK_EXTRA)).astype(BF16)
    write_gate(id_lanes[...], slot_lanes[...], weight_ref[...], score, gate_ref)


def write_gate(ids, slot, weight, score, out_ref):
    top_k, tokens = ids.shape
    row = lax.broadcasted_iota(jnp.int32, (LANES, tokens), 0)
    found = []
    for k in range(top_k):
        hit = jnp.where(ids[k : k + 1] == row, 1.0, 0.0).astype(BF16)
        mine = lax.dot_general(score, hit, FIRST, preferred_element_type=F32)
        found.append(
            jnp.sum(jnp.where(slot[k : k + 1] == row, mine, 0.0), axis=0, keepdims=True)
        )
    scale = (CHUNKS * LANES) ** (-0.5)
    value = jnp.concatenate(found, axis=0) * scale / weight.astype(F32)
    out_ref[...] = value.astype(BF16)


def probs_kernel(query_ref, key_ref, begin_ref, out_ref):
    scores = lax.dot_general(
        query_ref[...], key_ref[...], LAST, preferred_element_type=F32
    ) * HEAD_DIM ** (-0.5)
    here = lax.broadcasted_iota(jnp.int32, (SEQ, SEQ), 0)
    there = lax.broadcasted_iota(jnp.int32, (SEQ, SEQ), 1)
    visible = (there <= here) & (there >= begin_ref[...])
    masked = jnp.where(visible, scores, -1e30)
    top = jnp.max(masked, axis=1, keepdims=True)
    weights = jnp.where(visible, jnp.exp(masked - top), 0.0)
    out_ref[0, 0] = (weights / jnp.sum(weights, axis=1, keepdims=True)).astype(BF16)


def tail_kernel(
    sum_scale,
    resid_hbm,
    weight_hbm,
    attn_hbm,
    probs_hbm,
    query_hbm,
    key_hbm,
    value_hbm,
    dq_ref,
    dk_ref,
    dv_ref,
    out_ref,
    group,
    weight,
    attn,
    probs,
    query,
    key,
    value,
    grads,
    acc,
    pieces,
    arrived,
    load_sems,
    ring_send,
    ring_recv,
    side_send,
    side_recv,
    dp_send,
    dp_recv,
):
    ep, dp = lax.axis_index("ep"), lax.axis_index("dp")
    chips = lax.axis_size("ep") // 2
    dp_size = lax.axis_size("dp")
    chip, core = ep // 2, ep % 2
    tokens, width = resid_hbm.shape
    half = tokens // 2
    above = ((chip + 1) % chips) * 2 + core
    below = ((chip + chips - 1) % chips) * 2 + core
    across = ((chip + 2) % chips) * 2 + core
    sibling = chip * 2 + 1 - core

    barrier = pltpu.get_barrier_semaphore()
    for peer in (above, below, sibling):
        pl.semaphore_signal(barrier, inc=1, device_id=(peer, dp), device_id_type=MESH)
    for step in range(1, dp_size):
        pl.semaphore_signal(
            barrier, inc=1, device_id=(ep, (dp + step) % dp_size), device_id_type=MESH
        )

    loads = [
        pltpu.make_async_copy(source, target, load_sems.at[number])
        for number, (source, target) in enumerate(
            (
                (resid_hbm, group.at[pl.ds(pl.multiple_of(ep * tokens, tokens), tokens)]),
                (weight_hbm, weight),
                (attn_hbm, attn),
                (query_hbm, query),
                (key_hbm, key),
                (value_hbm, value),
                (probs_hbm, probs),
            )
        )
    ]
    for load in loads:
        load.start()
    loads[0].wait()
    pl.semaphore_wait(barrier, dp_size - 1 + 3)

    def part(owner, second):
        at = pl.multiple_of(owner * tokens + second * half, half)
        return group.at[pl.ds(at, half)]

    def ring(number, owner, second, target):
        return pltpu.make_async_remote_copy(
            src_ref=part(owner, second),
            dst_ref=part(owner, second),
            send_sem=ring_send.at[number],
            recv_sem=ring_recv.at[number],
            device_id=(target, dp),
            device_id_type=MESH,
        )

    def side(number, owner, second):
        return pltpu.make_async_remote_copy(
            src_ref=part(owner, second),
            dst_ref=part(owner, second),
            send_sem=side_send.at[number],
            recv_sem=side_recv.at[number],
            device_id=(sibling, dp),
            device_id_type=MESH,
        )

    up = [ring(0, ep, 0, above), ring(1, ep, 1, above)]
    down = [ring(3, ep, 0, below), ring(2, ep, 1, below)]
    own = [side(0, ep, 0), side(1, ep, 1)]
    for copy in (up[0], down[1], own[0], own[1], up[1], down[0]):
        copy.start()

    def matmuls(pair, last):
        at = pl.multiple_of(pair * 2 * tokens, 2 * tokens)
        mine = pl.ds(at, 2 * tokens)
        def add(step, carry):
            dest = (dp + 1 + step) % dp_size
            columns = pl.ds(pl.multiple_of(dest * tokens, tokens), tokens)
            product = lax.dot_general(
                group[mine, columns], attn[mine], FIRST, preferred_element_type=F32
            )
            if last is None:
                acc[dest] = product
            elif not last:
                acc[dest] = acc[dest] + product
            else:
                pieces[dest] = (acc[dest] + product).astype(BF16)
            return carry

        if not last:
            lax.fori_loop(0, dp_size, add, 0)
        else:
            for step in range(dp_size):
                add(step, 0)
                if step < dp_size - 1:
                    send_piece(step).start()
        grads[mine] = jnp.dot(group[mine], weight[...], preferred_element_type=F32).astype(BF16)

    def send_piece(step):
        dest = (dp + 1 + step) % dp_size
        return pltpu.make_async_remote_copy(
            src_ref=pieces.at[dest],
            dst_ref=arrived.at[dp],
            send_sem=dp_send.at[step],
            recv_sem=dp_recv.at[step],
            device_id=(ep, dest),
            device_id_type=MESH,
        )

    own[0].wait_recv()
    own[1].wait_recv()
    loads[1].wait()
    loads[2].wait()
    matmuls(chip, None)

    up[0].wait_recv()
    forward_up = ring(4, below, 0, above)
    forward_up.start()
    relay = [side(2, below, 0)]
    relay[0].start()
    down[1].wait_recv()
    forward_down = ring(5, above, 1, below)
    forward_down.start()
    relay.append(side(3, above, 1))
    relay[1].start()
    up[1].wait_recv()
    relay.append(side(4, below, 1))
    relay[2].start()
    down[0].wait_recv()
    relay.append(side(5, above, 0))
    relay[3].start()
    for copy in relay:
        copy.wait_recv()
    matmuls(below // 2, False)
    matmuls(above // 2, False)
    forward_up.wait_recv()
    relay.append(side(6, across, 0))
    relay[4].start()
    forward_down.wait_recv()
    relay.append(side(7, across, 1))
    relay[5].start()
    relay[4].wait_recv()
    relay[5].wait_recv()
    matmuls(across // 2, True)

    for load in loads[3:]:
        load.wait()
    heads = query.shape[1] // HEAD_DIM
    scale = HEAD_DIM ** (-0.5)

    def attend(number, carry):
        seq, head = number // heads, number % heads
        at = (
            pl.ds(pl.multiple_of(seq * SEQ, SEQ), SEQ),
            pl.ds(pl.multiple_of(head * HEAD_DIM, HEAD_DIM), HEAD_DIM),
        )
        grad = grads[at]
        weights = probs[number]
        delta = jnp.sum(grad.astype(F32) * attn[at].astype(F32), axis=1, keepdims=True)
        prob_grad = lax.dot_general(grad, value[at], LAST, preferred_element_type=F32)
        score_grad = (weights.astype(F32) * (prob_grad - delta)).astype(BF16)
        dq_ref[at] = (
            jnp.dot(score_grad, key[at], preferred_element_type=F32) * scale
        ).astype(BF16)
        dk_ref[at] = (
            lax.dot_general(score_grad, query[at], FIRST, preferred_element_type=F32) * scale
        ).astype(BF16)
        dv_ref[at] = lax.dot_general(weights, grad, FIRST, preferred_element_type=F32).astype(BF16)
        return carry

    lax.fori_loop(0, probs.shape[0], attend, 0)

    for step in range(dp_size - 1):
        send_piece(step).wait_recv()
    total = pieces[dp].astype(F32)
    for step in range(1, dp_size):
        total = total + arrived[(dp + step) % dp_size].astype(F32)
    out_ref[...] = (total * sum_scale).astype(BF16)
    for copy in up + down + own + relay + [forward_up, forward_down]:
        copy.wait_send()
    for step in range(dp_size - 1):
        send_piece(step).wait_send()


def publish_kernel(*refs):
    count = len(refs) // 2
    for i in range(count):
        refs[count + i][...] = refs[i][...]


def publish(arrays):
    steps = 2
    blocks = [
        pl.BlockSpec((a.shape[0] // steps, a.shape[1]), lambda i: (i, 0)) for a in arrays
    ]
    return call(
        publish_kernel,
        tuple(jax.ShapeDtypeStruct(a.shape, a.dtype) for a in arrays),
        moved=4000000,
        grid=(steps,),
        in_specs=blocks,
        out_specs=tuple(blocks),
    )(*arrays)


def per_device(
    hidden_state,
    out_grad,
    norm_gain,
    expert_ids,
    route_weight,
    w_gate,
    w_up,
    w_down,
    queries,
    keys,
    values,
    attn_out,
    out_weight,
    doc_start,
):
    tokens, width = hidden_state.shape
    top_k = expert_ids.shape[1]
    ff = w_gate.shape[2]
    dp_size = lax.axis_size("dp")
    experts = lax.axis_size("ep") * dp_size
    caps = 5 * tokens * top_k // (4 * experts)
    rows = experts * caps
    both = ("ep", "dp")
    swap = swap_matrix()
    hidden3 = hidden_state.reshape(tokens, CHUNKS, LANES)
    grad3 = out_grad.reshape(tokens, CHUNKS, LANES)
    gain2 = norm_gain.reshape(CHUNKS, LANES)

    ids_t, weight_t = expert_ids.T, route_weight.T
    table, scales, slots = call(
        functools.partial(slots_kernel, caps),
        (
            jax.ShapeDtypeStruct((16, experts), jnp.int32),
            jax.ShapeDtypeStruct((16, experts), F32),
            jax.ShapeDtypeStruct((top_k, tokens), jnp.int32),
        ),
        moved=300000,
    )(ids_t, weight_t)

    pack_block = pl.BlockSpec((DESTS * caps, CHUNKS, LANES), lambda i, *_: (i, 0, 0))

    def exchange(array):
        return lax.all_to_all(array, both, split_axis=0, concat_axis=0, tiled=True)

    def send(kernel, scalars, arrays, scratch):
        packed = call(
            kernel,
            jax.ShapeDtypeStruct((rows, CHUNKS, LANES), BF16),
            moved=6000000,
            grid_spec=pltpu.PrefetchScalarGridSpec(
                num_scalar_prefetch=len(scalars),
                grid=(experts // DESTS,),
                in_specs=[whole(a.shape) for a in arrays],
                out_specs=pack_block,
                scratch_shapes=scratch,
            ),
        )(*scalars, *arrays)
        return exchange(packed.reshape(experts, caps * 16, LANES)).reshape(rows * 16, LANES)

    table_scratch = [pltpu.VMEM((tokens + 1, CHUNKS, LANES), BF16)]
    got_rows = send(
        pack_rows_kernel, [table], [hidden_state, norm_gain.reshape(1, width), swap], table_scratch
    )
    got_grads = send(pack_grads_kernel, [table, scales], [grad3], [])

    group_len, head_cols = queries.shape
    head_count = head_cols // HEAD_DIM
    seq_count = group_len // SEQ
    head_block = pl.BlockSpec((SEQ, HEAD_DIM), lambda s, h: (s, h))
    probs_block = pl.BlockSpec((1, 1, SEQ, SEQ), lambda s, h: (s, h, 0, 0))
    probs = call(
        probs_kernel,
        jax.ShapeDtypeStruct((seq_count, head_count, SEQ, SEQ), BF16),
        flops=10**10,
        moved=5000000,
        grid=(seq_count, head_count),
        in_specs=[head_block, head_block, pl.BlockSpec((SEQ, 1), lambda s, h: (s, 0))],
        out_specs=probs_block,
    )(queries, keys, doc_start.reshape(group_len, 1))

    got_rows, probs, hidden3 = lax.optimization_barrier((got_rows, probs, hidden3))
    step_rows = SOURCES * caps
    steps = rows // step_rows
    flat_tiles = pl.BlockSpec((step_rows * 16, LANES), lambda i: (i, 0))
    wide = pl.BlockSpec((step_rows, width), lambda i: (i, 0))
    narrow = pl.BlockSpec((step_rows, ff), lambda i: (i, 0))
    w_in = whole((1, width, ff))
    w_out = whole((1, ff, width))
    narrow_shape = jax.ShapeDtypeStruct((rows, ff), BF16)
    wide_shape = jax.ShapeDtypeStruct((rows, width), BF16)
    rows_in, act, act_da, act_db = call(
        expert_up_kernel,
        (wide_shape, narrow_shape, narrow_shape, narrow_shape),
        flops=4 * rows * width * ff,
        moved=18000000,
        grid=(steps,),
        in_specs=[flat_tiles, whole((256, 256)), w_in, w_in],
        out_specs=(wide, narrow, narrow, narrow),
    )(got_rows, swap, w_gate, w_up)
    index = np.arange(step_rows)
    gather = jnp.asarray(index[None, :] // caps == np.arange(SOURCES)[:, None], BF16)
    spread = jnp.asarray(index[:, None] % caps == np.arange(LANES)[None, :], BF16)
    block_rows = caps * 16 + PACK_EXTRA
    scaled_grad, pre_grad, up_grad, send_back = call(
        functools.partial(expert_down_kernel, caps),
        (
            wide_shape,
            narrow_shape,
            narrow_shape,
            jax.ShapeDtypeStruct((experts, block_rows, LANES), BF16),
        ),
        flops=6 * rows * width * ff,
        moved=25000000,
        grid=(steps,),
        in_specs=[
            flat_tiles,
            whole((256, 256)),
            whole((SOURCES, step_rows)),
            whole((step_rows, LANES)),
            w_in,
            w_in,
            w_out,
            narrow,
            narrow,
            narrow,
        ],
        out_specs=(
            wide,
            narrow,
            narrow,
            pl.BlockSpec((SOURCES, block_rows, LANES), lambda i: (i, 0, 0)),
        ),
        scratch_shapes=[pltpu.VMEM((step_rows, width), BF16)],
    )(got_grads, swap, gather, spread, w_gate, w_up, w_down, act, act_da, act_db)
    back = exchange(send_back)
    grad_scale = (tokens * top_k) ** (-0.5)

    def weight_grad(left, right):
        product = lax.dot_general(left, right, FIRST, preferred_element_type=F32)
        return (product * grad_scale).astype(BF16)[None]

    grad_gate_w = weight_grad(rows_in, pre_grad)
    grad_up_w = weight_grad(rows_in, up_grad)
    grad_down_w = weight_grad(act, scaled_grad)

    back, grad_gate_w, grad_up_w, grad_down_w = lax.optimization_barrier(
        (back, grad_gate_w, grad_up_w, grad_down_w)
    )
    residual_grad, gate_grad = call(
        combine_kernel,
        (
            jax.ShapeDtypeStruct((tokens, width), BF16),
            jax.ShapeDtypeStruct((top_k, tokens), BF16),
        ),
        moved=8000000,
        grid_spec=pltpu.PrefetchScalarGridSpec(
            num_scalar_prefetch=2,
            grid=(1,),
            in_specs=[
                whole(back.shape),
                whole((tokens, CHUNKS, LANES)),
                whole((tokens, CHUNKS, LANES)),
                whole((CHUNKS, LANES)),
                whole((256, 256)),
                whole((top_k, tokens)),
                whole((top_k, tokens)),
                whole((top_k, tokens)),
            ],
            out_specs=(whole((tokens, width)), whole((top_k, tokens))),
            scratch_shapes=[
                pltpu.VMEM((tokens, CHUNKS, LANES), F32),
                pltpu.VMEM((tokens * CHUNKS, LANES), BF16),
            ],
        ),
    )(ids_t, slots, back, hidden3, grad3, gain2, swap, ids_t, slots, weight_t)
    gate_grad = gate_grad.T

    any_spec = pl.BlockSpec(memory_space=pl.ANY)
    vmem_spec = pl.BlockSpec(memory_space=pltpu.VMEM)
    head_shape = jax.ShapeDtypeStruct((group_len, head_cols), BF16)
    head_vmem = pltpu.VMEM((group_len, head_cols), BF16)
    piece_shape = (dp_size, width // dp_size, head_cols)
    tail_results = pl.pallas_call(
        functools.partial(tail_kernel, (group_len * dp_size) ** (-0.5)),
        out_shape=(
            head_shape,
            head_shape,
            head_shape,
            jax.ShapeDtypeStruct(piece_shape[1:], BF16),
        ),
        in_specs=[any_spec] * 7,
        out_specs=(vmem_spec,) * 4,
        scratch_shapes=[
            pltpu.VMEM((group_len, width), BF16),
            pltpu.VMEM((width, head_cols), BF16),
            head_vmem,
            pltpu.VMEM((seq_count * head_count, SEQ, SEQ), BF16),
            head_vmem,
            head_vmem,
            head_vmem,
            head_vmem,
            pltpu.VMEM(piece_shape, F32),
            pltpu.VMEM(piece_shape, BF16),
            pltpu.VMEM(piece_shape, BF16),
            pltpu.SemaphoreType.DMA((7,)),
            pltpu.SemaphoreType.DMA((6,)),
            pltpu.SemaphoreType.DMA((6,)),
            pltpu.SemaphoreType.DMA((8,)),
            pltpu.SemaphoreType.DMA((8,)),
            pltpu.SemaphoreType.DMA((dp_size - 1,)),
            pltpu.SemaphoreType.DMA((dp_size - 1,)),
        ],
        compiler_params=pltpu.CompilerParams(
            collective_id=0, has_side_effects=True, vmem_limit_bytes=VMEM_LIMIT
        ),
        cost_estimate=pl.CostEstimate(
            flops=4 * 10**9, bytes_accessed=20000000, transcendentals=0
        ),
    )(
        residual_grad,
        out_weight,
        attn_out,
        probs.reshape(seq_count * head_count, SEQ, SEQ),
        queries,
        keys,
        values,
    )
    query_grad, key_grad, value_grad, out_weight_grad = publish(tail_results)
    return (
        gate_grad,
        grad_gate_w,
        grad_up_w,
        grad_down_w,
        residual_grad,
        out_weight_grad,
        query_grad,
        key_grad,
        value_grad,
    )


def solution(mesh):
    tokens = P(("dp", "ep"), None)
    expert = P(("ep", "dp"), None, None)
    heads = P("dp", "ep")
    return jax.shard_map(
        per_device,
        mesh=mesh,
        in_specs=(
            tokens,
            tokens,
            P(),
            tokens,
            tokens,
            expert,
            expert,
            expert,
            heads,
            heads,
            heads,
            heads,
            P(None, "ep"),
            P("dp"),
        ),
        out_specs=(tokens, expert, expert, expert, tokens, heads, heads, heads, heads),
        check_vma=False,
    )
```

```python
import functools

import jax
import jax.numpy as jnp
import numpy as np
from jax import lax
from jax.experimental import pallas as pl
from jax.experimental.pallas import tpu as pltpu
from jax.sharding import PartitionSpec as P

HEAD_DIM = 128
SEQ = 512
EPS = 1e-06
LANES = 128
CHUNKS = 16
F32 = jnp.float32
BF16 = jnp.bfloat16
MESH = pl.DeviceIdType.MESH
LAST = (((1,), (1,)), ((), ()))
FIRST = (((0,), (0,)), ((), ()))
PACK_EXTRA = 8
DESTS = 32
SOURCES = 32
VMEM_LIMIT = 56 * 1024 * 1024


def swap_matrix():
    index = np.arange(256)
    matrix = np.zeros((256, 256), np.float32)
    matrix[(index % 16) * 16 + index // 16, index] = 1.0
    return jnp.asarray(matrix, BF16)


def call(kernel, out_shape, flops=0, moved=0, **kwargs):
    return pl.pallas_call(
        kernel,
        out_shape=out_shape,
        compiler_params=pltpu.CompilerParams(vmem_limit_bytes=VMEM_LIMIT),
        cost_estimate=pl.CostEstimate(flops=flops, bytes_accessed=moved, transcendentals=0),
        **kwargs,
    )


def whole(shape):
    return pl.BlockSpec(shape, lambda *_: (0,) * len(shape))


def tiles_to_rows(get_tiles, swap, out_ref, groups):
    for group in range(groups):
        pair = jnp.concatenate([get_tiles(2 * group), get_tiles(2 * group + 1)], axis=1)
        turned = jnp.dot(swap, pair, preferred_element_type=F32).astype(BF16)
        for chunk in range(CHUNKS):
            cols = slice(chunk * LANES, (chunk + 1) * LANES)
            rows = turned[chunk * 16 : (chunk + 1) * 16]
            out_ref[group * 32 : group * 32 + 16, cols] = rows[:, :LANES]
            out_ref[group * 32 + 16 : group * 32 + 32, cols] = rows[:, LANES:]


def turn_rows(rows, swap):
    halves = [
        jnp.concatenate(
            [
                rows[side * 16 : side * 16 + 16, chunk * LANES : (chunk + 1) * LANES]
                for chunk in range(CHUNKS)
            ],
            axis=0,
        )
        for side in range(2)
    ]
    pair = jnp.concatenate(halves, axis=1)
    return jnp.dot(swap, pair, preferred_element_type=F32).astype(BF16)


def slots_kernel(caps, ids_ref, weight_ref, table_ref, scale_ref, slot_ref):
    top_k, tokens = ids_ref.shape
    experts = LANES
    lane = lax.broadcasted_iota(jnp.int32, (experts, tokens), 1)
    row = lax.broadcasted_iota(jnp.int32, (experts, tokens), 0)
    ids = ids_ref[...]
    weight = weight_ref[...].astype(F32)
    chosen = jnp.zeros((experts, tokens), F32)
    weights = jnp.zeros((experts, tokens), F32)
    for k in range(top_k):
        hit = ids[k : k + 1] == row
        chosen = jnp.where(hit, 1.0, chosen)
        weights = jnp.where(hit, weight[k : k + 1], weights)
    upper = jnp.where(row < lane, 1.0, 0.0).astype(BF16)
    counts = jnp.dot(chosen.astype(BF16), upper, preferred_element_type=F32)
    table = jnp.zeros((experts, LANES), F32)
    scales = jnp.zeros((experts, LANES), F32)
    from_end = (lane - tokens).astype(F32)
    for place in range(caps):
        mask = (chosen > 0.5) & (jnp.abs(counts - place) < 0.5)
        token = jnp.sum(jnp.where(mask, from_end, 0.0), axis=1, keepdims=True) + tokens
        scale = jnp.sum(jnp.where(mask, weights, 0.0), axis=1, keepdims=True)
        table = jnp.where(lane == place, token, table)
        scales = jnp.where(lane == place, scale, scales)
    table_ref[...] = table.T[:16].astype(jnp.int32)
    scale_ref[...] = scales.T[:16]
    slot_ref[...] = jnp.concatenate(
        [
            jnp.sum(jnp.where(ids[k : k + 1] == row, counts, 0.0), axis=0, keepdims=True)
            for k in range(top_k)
        ],
        axis=0,
    ).astype(jnp.int32)


def pack_rows_kernel(table_ref, hidden_ref, gain_ref, swap_ref, out_ref, normed):
    tokens, width = hidden_ref.shape
    step = pl.program_id(0)
    caps = out_ref.shape[0] // DESTS

    @pl.when(step == 0)
    def _():
        gain = gain_ref[...].astype(F32)
        gain = jnp.concatenate([gain[chunk : chunk + 1] for chunk in range(CHUNKS)], axis=1)
        swap = swap_ref[...]
        for start in range(0, tokens, 32):
            hidden = hidden_ref[start : start + 32].astype(F32)
            mean = jnp.sum(hidden * hidden, axis=1, keepdims=True) * (1.0 / width)
            low = (hidden * lax.rsqrt(mean + EPS) * gain).astype(BF16)
            turned = turn_rows(low, swap)
            for side in range(2):
                for inner in range(16):
                    normed[start + side * 16 + inner] = turned[
                        inner * 16 : (inner + 1) * 16, side * LANES : (side + 1) * LANES
                    ]
        normed[tokens] = jnp.zeros((CHUNKS, LANES), BF16)

    def fill(dest, carry):
        for place in range(caps):
            out_ref[dest * caps + place] = normed[table_ref[place, step * DESTS + dest]]
        return carry

    lax.fori_loop(0, DESTS, fill, 0, unroll=2)


def pack_grads_kernel(table_ref, scale_ref, grad_ref, out_ref):
    tokens = grad_ref.shape[0]
    step = pl.program_id(0)
    caps = out_ref.shape[0] // DESTS

    def fill(dest, carry):
        for place in range(caps):
            at = step * DESTS + dest
            token = jnp.minimum(table_ref[place, at], tokens - 1)
            scale = scale_ref[place, at]
            out_ref[dest * caps + place] = (grad_ref[token].astype(F32) * scale).astype(BF16)
        return carry

    lax.fori_loop(0, DESTS, fill, 0, unroll=2)


def expert_up_kernel(tile_ref, swap_ref, gate_w_ref, up_w_ref, row_ref, act_ref, da_ref, db_ref):
    rows = row_ref.shape[0]
    tiles_to_rows(
        lambda i: tile_ref[i * 256 : (i + 1) * 256], swap_ref[...], row_ref, rows // 32
    )
    gate = jnp.dot(row_ref[...], gate_w_ref[0], preferred_element_type=F32)
    up = jnp.dot(row_ref[...], up_w_ref[0], preferred_element_type=F32)
    sig = 1.0 / (1.0 + jnp.exp(-gate))
    silu = gate * sig
    act_ref[...] = (silu * up).astype(BF16)
    da_ref[...] = (up * sig * (1.0 + gate * (1.0 - sig))).astype(BF16)
    db_ref[...] = silu.astype(BF16)


def expert_down_kernel(
    caps,
    tile_ref,
    swap_ref,
    gather_ref,
    spread_ref,
    gate_w_ref,
    up_w_ref,
    down_w_ref,
    act_ref,
    da_ref,
    db_ref,
    grad_ref,
    pre_ref,
    upg_ref,
    back_ref,
    rowg,
):
    rows = grad_ref.shape[0]
    swap = swap_ref[...]
    tiles_to_rows(lambda i: tile_ref[i * 256 : (i + 1) * 256], swap, grad_ref, rows // 32)
    act_grad = lax.dot_general(grad_ref[...], down_w_ref[0], LAST, preferred_element_type=F32)
    pre = (act_grad * da_ref[...].astype(F32)).astype(BF16)
    upg = (act_grad * db_ref[...].astype(F32)).astype(BF16)
    pre_ref[...] = pre
    upg_ref[...] = upg
    score = jnp.sum(act_grad * act_ref[...].astype(F32), axis=1, keepdims=True)
    placed = jnp.dot(
        gather_ref[...],
        (score * spread_ref[...].astype(F32)).astype(BF16),
        preferred_element_type=F32,
    ).astype(BF16)
    rowg[...] = (
        lax.dot_general(pre, gate_w_ref[0], LAST, preferred_element_type=F32)
        + lax.dot_general(upg, up_w_ref[0], LAST, preferred_element_type=F32)
    ).astype(BF16)
    for group in range(rows // 32):
        halves = []
        for side in range(2):
            at = group * 32 + side * 16
            halves.append(
                jnp.concatenate(
                    [
                        rowg[at : at + 16, chunk * LANES : (chunk + 1) * LANES]
                        for chunk in range(CHUNKS)
                    ],
                    axis=0,
                )
            )
        turned = jnp.dot(
            swap, jnp.concatenate(halves, axis=1), preferred_element_type=F32
        ).astype(BF16)
        for side in range(2):
            for inner in range(16):
                row = group * 32 + side * 16 + inner
                place = (row % caps) * 16
                back_ref[row // caps, place : place + 16, :] = turned[
                    inner * 16 : (inner + 1) * 16, side * LANES : (side + 1) * LANES
                ]
    for source in range(rows // caps):
        back_ref[source, caps * 16 : caps * 16 + PACK_EXTRA, :] = jnp.broadcast_to(
            placed[source : source + 1], (PACK_EXTRA, LANES)
        )


def combine_kernel(
    ids_ref,
    slot_ref,
    back_ref,
    hidden_ref,
    grad_ref,
    gain_ref,
    swap_ref,
    out_ref,
    score_ref,
    total,
    tiles,
):
    top_k, tokens = ids_ref.shape

    def gather(token, carry):
        acc = jnp.zeros((CHUNKS, LANES), F32)
        for k in range(top_k):
            at = pl.multiple_of(slot_ref[k, token] * 16, 16)
            acc = acc + back_ref[ids_ref[k, token], pl.ds(at, 16), :].astype(F32)
        total[token] = acc
        return carry

    lax.fori_loop(0, tokens, gather, 0, unroll=4)
    gain = gain_ref[...].astype(F32)[None]
    share = 1.0 / (CHUNKS * LANES)

    def mean(value):
        return (
            jnp.sum(jnp.sum(value, axis=2, keepdims=True), axis=1, keepdims=True) * share
        )

    for start in range(0, tokens, 16):
        hidden = hidden_ref[start : start + 16].astype(F32)
        inv_rms = lax.rsqrt(mean(hidden * hidden) + EPS)
        unit = hidden * inv_rms
        scaled = total[start : start + 16] * gain
        residual = grad_ref[start : start + 16].astype(F32) + inv_rms * (
            scaled - unit * mean(scaled * unit)
        )
        tiles[start * 16 : start * 16 + 256] = residual.astype(BF16).reshape(256, LANES)
    tiles_to_rows(
        lambda i: tiles[i * 256 : (i + 1) * 256], swap_ref[...], out_ref, tokens // 32
    )
    extra = back_ref[:, back_ref.shape[1] - PACK_EXTRA :, :].astype(F32)
    score_ref[...] = (jnp.sum(extra, axis=1) * (1.0 / PACK_EXTRA)).astype(BF16)


def write_gate(ids, slot, weight, score, out_ref):
    top_k, tokens = ids.shape
    row = lax.broadcasted_iota(jnp.int32, (LANES, tokens), 0)
    found = []
    for k in range(top_k):
        hit = jnp.where(ids[k : k + 1] == row, 1.0, 0.0).astype(BF16)
        mine = lax.dot_general(score, hit, FIRST, preferred_element_type=F32)
        found.append(
            jnp.sum(jnp.where(slot[k : k + 1] == row, mine, 0.0), axis=0, keepdims=True)
        )
    scale = (CHUNKS * LANES) ** (-0.5)
    value = jnp.concatenate(found, axis=0) * scale / weight.astype(F32)
    out_ref[...] = value.astype(BF16)


def probs_kernel(query_ref, key_ref, begin_ref, out_ref):
    scores = lax.dot_general(
        query_ref[...], key_ref[...], LAST, preferred_element_type=F32
    ) * HEAD_DIM ** (-0.5)
    here = lax.broadcasted_iota(jnp.int32, (SEQ, SEQ), 0)
    there = lax.broadcasted_iota(jnp.int32, (SEQ, SEQ), 1)
    visible = (there <= here) & (there >= begin_ref[...])
    masked = jnp.where(visible, scores, -1e30)
    top = jnp.max(masked, axis=1, keepdims=True)
    weights = jnp.where(visible, jnp.exp(masked - top), 0.0)
    out_ref[0, 0] = (weights / jnp.sum(weights, axis=1, keepdims=True)).astype(BF16)


def tail_kernel(
    sum_scale,
    resid_hbm,
    weight_hbm,
    attn_hbm,
    probs_hbm,
    query_hbm,
    key_hbm,
    value_hbm,
    id_ref,
    slot_ref,
    pair_ref,
    score_ref,
    dq_ref,
    dk_ref,
    dv_ref,
    out_ref,
    gate_ref,
    group,
    weight,
    attn,
    probs,
    query,
    key,
    value,
    grads,
    acc,
    pieces,
    arrived,
    load_sems,
    ring_send,
    ring_recv,
    side_send,
    side_recv,
    dp_send,
    dp_recv,
):
    ep, dp = lax.axis_index("ep"), lax.axis_index("dp")
    chips = lax.axis_size("ep") // 2
    dp_size = lax.axis_size("dp")
    chip, core = ep // 2, ep % 2
    tokens, width = resid_hbm.shape
    half = tokens // 2
    above = ((chip + 1) % chips) * 2 + core
    below = ((chip + chips - 1) % chips) * 2 + core
    across = ((chip + 2) % chips) * 2 + core
    sibling = chip * 2 + 1 - core

    barrier = pltpu.get_barrier_semaphore()
    for peer in (above, below, sibling):
        pl.semaphore_signal(barrier, inc=1, device_id=(peer, dp), device_id_type=MESH)
    for step in range(1, dp_size):
        pl.semaphore_signal(
            barrier, inc=1, device_id=(ep, (dp + step) % dp_size), device_id_type=MESH
        )

    loads = [
        pltpu.make_async_copy(source, target, load_sems.at[number])
        for number, (source, target) in enumerate(
            (
                (resid_hbm, group.at[pl.ds(pl.multiple_of(ep * tokens, tokens), tokens)]),
                (weight_hbm, weight),
                (attn_hbm, attn),
                (query_hbm, query),
                (key_hbm, key),
                (value_hbm, value),
                (probs_hbm, probs),
            )
        )
    ]
    for load in loads:
        load.start()
    pl.semaphore_wait(barrier, dp_size - 1 + 3)

    def part(owner, second):
        at = pl.multiple_of(owner * tokens + second * half, half)
        return group.at[pl.ds(at, half)]

    def mine_at(second):
        return resid_hbm.at[pl.ds(second * half, half)]

    def ring(number, owner, second, target, source=None):
        return pltpu.make_async_remote_copy(
            src_ref=part(owner, second) if source is None else source,
            dst_ref=part(owner, second),
            send_sem=ring_send.at[number],
            recv_sem=ring_recv.at[number],
            device_id=(target, dp),
            device_id_type=MESH,
        )

    def side(number, owner, second, source=None):
        return pltpu.make_async_remote_copy(
            src_ref=part(owner, second) if source is None else source,
            dst_ref=part(owner, second),
            send_sem=side_send.at[number],
            recv_sem=side_recv.at[number],
            device_id=(sibling, dp),
            device_id_type=MESH,
        )

    first, second = mine_at(0), mine_at(1)
    up = [ring(0, ep, 0, above, first), ring(1, ep, 1, above, second)]
    down = [ring(3, ep, 0, below, first), ring(2, ep, 1, below, second)]
    own = [side(0, ep, 0, first), side(1, ep, 1, second)]
    for copy in (up[0], down[1], own[0], own[1], up[1], down[0]):
        copy.start()

    def matmuls(pair, last):
        at = pl.multiple_of(pair * 2 * tokens, 2 * tokens)
        mine = pl.ds(at, 2 * tokens)
        def add(step, carry):
            dest = (dp + 1 + step) % dp_size
            columns = pl.ds(pl.multiple_of(dest * tokens, tokens), tokens)
            product = lax.dot_general(
                group[mine, columns], attn[mine], FIRST, preferred_element_type=F32
            )
            if last is None:
                acc[dest] = product
            elif not last:
                acc[dest] = acc[dest] + product
            else:
                pieces[dest] = (acc[dest] + product).astype(BF16)
            return carry

        if not last:
            lax.fori_loop(0, dp_size, add, 0)
        else:
            for step in range(dp_size):
                add(step, 0)
                if step < dp_size - 1:
                    send_piece(step).start()
        grads[mine] = jnp.dot(group[mine], weight[...], preferred_element_type=F32).astype(BF16)

    def send_piece(step):
        dest = (dp + 1 + step) % dp_size
        return pltpu.make_async_remote_copy(
            src_ref=pieces.at[dest],
            dst_ref=arrived.at[dp],
            send_sem=dp_send.at[step],
            recv_sem=dp_recv.at[step],
            device_id=(ep, dest),
            device_id_type=MESH,
        )

    write_gate(id_ref[...], slot_ref[...], pair_ref[...], score_ref[...], gate_ref)
    loads[0].wait()
    own[0].wait_recv()
    own[1].wait_recv()
    loads[1].wait()
    loads[2].wait()
    matmuls(chip, None)

    up[0].wait_recv()
    forward_up = ring(4, below, 0, above)
    forward_up.start()
    relay = [side(2, below, 0)]
    relay[0].start()
    down[1].wait_recv()
    forward_down = ring(5, above, 1, below)
    forward_down.start()
    relay.append(side(3, above, 1))
    relay[1].start()
    up[1].wait_recv()
    relay.append(side(4, below, 1))
    relay[2].start()
    down[0].wait_recv()
    relay.append(side(5, above, 0))
    relay[3].start()
    for copy in relay:
        copy.wait_recv()
    matmuls(below // 2, False)
    matmuls(above // 2, False)
    forward_up.wait_recv()
    relay.append(side(6, across, 0))
    relay[4].start()
    forward_down.wait_recv()
    relay.append(side(7, across, 1))
    relay[5].start()
    relay[4].wait_recv()
    relay[5].wait_recv()
    matmuls(across // 2, True)

    for load in loads[3:]:
        load.wait()
    heads = query.shape[1] // HEAD_DIM
    scale = HEAD_DIM ** (-0.5)

    def attend(number, carry):
        seq, head = number // heads, number % heads
        at = (
            pl.ds(pl.multiple_of(seq * SEQ, SEQ), SEQ),
            pl.ds(pl.multiple_of(head * HEAD_DIM, HEAD_DIM), HEAD_DIM),
        )
        grad = grads[at]
        weights = probs[number]
        delta = jnp.sum(grad.astype(F32) * attn[at].astype(F32), axis=1, keepdims=True)
        prob_grad = lax.dot_general(grad, value[at], LAST, preferred_element_type=F32)
        score_grad = (weights.astype(F32) * (prob_grad - delta)).astype(BF16)
        dq_ref[at] = (
            jnp.dot(score_grad, key[at], preferred_element_type=F32) * scale
        ).astype(BF16)
        dk_ref[at] = (
            lax.dot_general(score_grad, query[at], FIRST, preferred_element_type=F32) * scale
        ).astype(BF16)
        dv_ref[at] = lax.dot_general(weights, grad, FIRST, preferred_element_type=F32).astype(BF16)
        return carry

    lax.fori_loop(0, probs.shape[0], attend, 0)

    for step in range(dp_size - 1):
        send_piece(step).wait_recv()
    total = pieces[dp].astype(F32)
    for step in range(1, dp_size):
        total = total + arrived[(dp + step) % dp_size].astype(F32)
    out_ref[...] = (total * sum_scale).astype(BF16)
    for copy in up + down + own + relay + [forward_up, forward_down]:
        copy.wait_send()
    for step in range(dp_size - 1):
        send_piece(step).wait_send()


def publish_kernel(*refs):
    count = len(refs) // 2
    for i in range(count):
        refs[count + i][...] = refs[i][...]


def publish(arrays):
    steps = 2
    blocks = [
        pl.BlockSpec((a.shape[0] // steps, a.shape[1]), lambda i: (i, 0))
        if a.shape[0] % (16 * steps) == 0
        else whole(a.shape)
        for a in arrays
    ]
    return call(
        publish_kernel,
        tuple(jax.ShapeDtypeStruct(a.shape, a.dtype) for a in arrays),
        moved=4000000,
        grid=(steps,),
        in_specs=blocks,
        out_specs=tuple(blocks),
    )(*arrays)


def per_device(
    hidden_state,
    out_grad,
    norm_gain,
    expert_ids,
    route_weight,
    w_gate,
    w_up,
    w_down,
    queries,
    keys,
    values,
    attn_out,
    out_weight,
    doc_start,
):
    tokens, width = hidden_state.shape
    top_k = expert_ids.shape[1]
    ff = w_gate.shape[2]
    dp_size = lax.axis_size("dp")
    experts = lax.axis_size("ep") * dp_size
    caps = 5 * tokens * top_k // (4 * experts)
    rows = experts * caps
    both = ("ep", "dp")
    swap = swap_matrix()
    hidden3 = hidden_state.reshape(tokens, CHUNKS, LANES)
    grad3 = out_grad.reshape(tokens, CHUNKS, LANES)
    gain2 = norm_gain.reshape(CHUNKS, LANES)

    ids_t, weight_t = expert_ids.T, route_weight.T
    table, scales, slots = call(
        functools.partial(slots_kernel, caps),
        (
            jax.ShapeDtypeStruct((16, experts), jnp.int32),
            jax.ShapeDtypeStruct((16, experts), F32),
            jax.ShapeDtypeStruct((top_k, tokens), jnp.int32),
        ),
        moved=300000,
    )(ids_t, weight_t)

    pack_block = pl.BlockSpec((DESTS * caps, CHUNKS, LANES), lambda i, *_: (i, 0, 0))

    def exchange(array):
        return lax.all_to_all(array, both, split_axis=0, concat_axis=0, tiled=True)

    def send(kernel, scalars, arrays, scratch):
        packed = call(
            kernel,
            jax.ShapeDtypeStruct((rows, CHUNKS, LANES), BF16),
            moved=6000000,
            grid_spec=pltpu.PrefetchScalarGridSpec(
                num_scalar_prefetch=len(scalars),
                grid=(experts // DESTS,),
                in_specs=[whole(a.shape) for a in arrays],
                out_specs=pack_block,
                scratch_shapes=scratch,
            ),
        )(*scalars, *arrays)
        return exchange(packed.reshape(experts, caps * 16, LANES)).reshape(rows * 16, LANES)

    table_scratch = [pltpu.VMEM((tokens + 1, CHUNKS, LANES), BF16)]
    got_rows = send(
        pack_rows_kernel, [table], [hidden_state, gain2, swap], table_scratch
    )
    got_grads = send(pack_grads_kernel, [table, scales], [grad3], [])

    group_len, head_cols = queries.shape
    head_count = head_cols // HEAD_DIM
    seq_count = group_len // SEQ
    head_block = pl.BlockSpec((SEQ, HEAD_DIM), lambda s, h: (s, h))
    probs_block = pl.BlockSpec((1, 1, SEQ, SEQ), lambda s, h: (s, h, 0, 0))
    probs = call(
        probs_kernel,
        jax.ShapeDtypeStruct((seq_count, head_count, SEQ, SEQ), BF16),
        flops=10**10,
        moved=5000000,
        grid=(seq_count, head_count),
        in_specs=[head_block, head_block, pl.BlockSpec((SEQ, 1), lambda s, h: (s, 0))],
        out_specs=probs_block,
    )(queries, keys, doc_start.reshape(group_len, 1))

    got_rows, probs, hidden3 = lax.optimization_barrier((got_rows, probs, hidden3))
    step_rows = SOURCES * caps
    steps = rows // step_rows
    flat_tiles = pl.BlockSpec((step_rows * 16, LANES), lambda i: (i, 0))
    wide = pl.BlockSpec((step_rows, width), lambda i: (i, 0))
    narrow = pl.BlockSpec((step_rows, ff), lambda i: (i, 0))
    w_in = whole((1, width, ff))
    w_out = whole((1, ff, width))
    narrow_shape = jax.ShapeDtypeStruct((rows, ff), BF16)
    wide_shape = jax.ShapeDtypeStruct((rows, width), BF16)
    rows_in, act, act_da, act_db = call(
        expert_up_kernel,
        (wide_shape, narrow_shape, narrow_shape, narrow_shape),
        flops=4 * rows * width * ff,
        moved=18000000,
        grid=(steps,),
        in_specs=[flat_tiles, whole((256, 256)), w_in, w_in],
        out_specs=(wide, narrow, narrow, narrow),
    )(got_rows, swap, w_gate, w_up)
    index = np.arange(step_rows)
    gather = jnp.asarray(index[None, :] // caps == np.arange(SOURCES)[:, None], BF16)
    spread = jnp.asarray(index[:, None] % caps == np.arange(LANES)[None, :], BF16)
    block_rows = caps * 16 + PACK_EXTRA
    scaled_grad, pre_grad, up_grad, send_back = call(
        functools.partial(expert_down_kernel, caps),
        (
            wide_shape,
            narrow_shape,
            narrow_shape,
            jax.ShapeDtypeStruct((experts, block_rows, LANES), BF16),
        ),
        flops=6 * rows * width * ff,
        moved=25000000,
        grid=(steps,),
        in_specs=[
            flat_tiles,
            whole((256, 256)),
            whole((SOURCES, step_rows)),
            whole((step_rows, LANES)),
            w_in,
            w_in,
            w_out,
            narrow,
            narrow,
            narrow,
        ],
        out_specs=(
            wide,
            narrow,
            narrow,
            pl.BlockSpec((SOURCES, block_rows, LANES), lambda i: (i, 0, 0)),
        ),
        scratch_shapes=[pltpu.VMEM((step_rows, width), BF16)],
    )(got_grads, swap, gather, spread, w_gate, w_up, w_down, act, act_da, act_db)
    back = exchange(send_back)
    grad_scale = (tokens * top_k) ** (-0.5)

    def weight_grad(left, right):
        product = lax.dot_general(left, right, FIRST, preferred_element_type=F32)
        return (product * grad_scale).astype(BF16)[None]

    grad_gate_w = weight_grad(rows_in, pre_grad)
    grad_up_w = weight_grad(rows_in, up_grad)
    grad_down_w = weight_grad(act, scaled_grad)

    back, grad_gate_w, grad_up_w, grad_down_w = lax.optimization_barrier(
        (back, grad_gate_w, grad_up_w, grad_down_w)
    )
    residual_grad, scores = call(
        combine_kernel,
        (
            jax.ShapeDtypeStruct((tokens, width), BF16),
            jax.ShapeDtypeStruct((experts, LANES), BF16),
        ),
        moved=8000000,
        grid_spec=pltpu.PrefetchScalarGridSpec(
            num_scalar_prefetch=2,
            grid=(1,),
            in_specs=[
                whole(back.shape),
                whole((tokens, CHUNKS, LANES)),
                whole((tokens, CHUNKS, LANES)),
                whole((CHUNKS, LANES)),
                whole((256, 256)),
            ],
            out_specs=(whole((tokens, width)), whole((experts, LANES))),
            scratch_shapes=[
                pltpu.VMEM((tokens, CHUNKS, LANES), F32),
                pltpu.VMEM((tokens * CHUNKS, LANES), BF16),
            ],
        ),
    )(ids_t, slots, back, hidden3, grad3, gain2, swap)
    any_spec = pl.BlockSpec(memory_space=pl.ANY)
    vmem_spec = pl.BlockSpec(memory_space=pltpu.VMEM)
    head_shape = jax.ShapeDtypeStruct((group_len, head_cols), BF16)
    head_vmem = pltpu.VMEM((group_len, head_cols), BF16)
    piece_shape = (dp_size, width // dp_size, head_cols)
    tail_results = pl.pallas_call(
        functools.partial(tail_kernel, (group_len * dp_size) ** (-0.5)),
        out_shape=(
            head_shape,
            head_shape,
            head_shape,
            jax.ShapeDtypeStruct(piece_shape[1:], BF16),
            jax.ShapeDtypeStruct((top_k, tokens), BF16),
        ),
        in_specs=[any_spec] * 7 + [vmem_spec] * 4,
        out_specs=(vmem_spec,) * 5,
        scratch_shapes=[
            pltpu.VMEM((group_len, width), BF16),
            pltpu.VMEM((width, head_cols), BF16),
            head_vmem,
            pltpu.VMEM((seq_count * head_count, SEQ, SEQ), BF16),
            head_vmem,
            head_vmem,
            head_vmem,
            head_vmem,
            pltpu.VMEM(piece_shape, F32),
            pltpu.VMEM(piece_shape, BF16),
            pltpu.VMEM(piece_shape, BF16),
            pltpu.SemaphoreType.DMA((7,)),
            pltpu.SemaphoreType.DMA((6,)),
            pltpu.SemaphoreType.DMA((6,)),
            pltpu.SemaphoreType.DMA((8,)),
            pltpu.SemaphoreType.DMA((8,)),
            pltpu.SemaphoreType.DMA((dp_size - 1,)),
            pltpu.SemaphoreType.DMA((dp_size - 1,)),
        ],
        compiler_params=pltpu.CompilerParams(
            collective_id=0, has_side_effects=True, vmem_limit_bytes=VMEM_LIMIT
        ),
        cost_estimate=pl.CostEstimate(
            flops=4 * 10**9, bytes_accessed=20000000, transcendentals=0
        ),
    )(
        residual_grad,
        out_weight,
        attn_out,
        probs.reshape(seq_count * head_count, SEQ, SEQ),
        queries,
        keys,
        values,
        ids_t,
        slots,
        weight_t,
        scores,
    )
    query_grad, key_grad, value_grad, out_weight_grad, gate_grad = publish(tail_results)
    return (
        gate_grad.T,
        grad_gate_w,
        grad_up_w,
        grad_down_w,
        residual_grad,
        out_weight_grad,
        query_grad,
        key_grad,
        value_grad,
    )


def solution(mesh):
    tokens = P(("dp", "ep"), None)
    expert = P(("ep", "dp"), None, None)
    heads = P("dp", "ep")
    return jax.shard_map(
        per_device,
        mesh=mesh,
        in_specs=(
            tokens,
            tokens,
            P(),
            tokens,
            tokens,
            expert,
            expert,
            expert,
            heads,
            heads,
            heads,
            heads,
            P(None, "ep"),
            P("dp"),
        ),
        out_specs=(tokens, expert, expert, expert, tokens, heads, heads, heads, heads),
        check_vma=False,
    )
```

```python
import functools

import jax
import jax.numpy as jnp
import numpy as np
from jax import lax
from jax.experimental import pallas as pl
from jax.experimental.pallas import tpu as pltpu
from jax.sharding import PartitionSpec as P

HEAD_DIM = 128
SEQ = 512
EPS = 1e-06
LANES = 128
CHUNKS = 16
F32 = jnp.float32
BF16 = jnp.bfloat16
MESH = pl.DeviceIdType.MESH
LAST = (((1,), (1,)), ((), ()))
FIRST = (((0,), (0,)), ((), ()))
PACK_EXTRA = 8
DESTS = 32
SOURCES = 32
VMEM_LIMIT = 56 * 1024 * 1024


def swap_matrix():
    index = np.arange(256)
    matrix = np.zeros((256, 256), np.float32)
    matrix[(index % 16) * 16 + index // 16, index] = 1.0
    return jnp.asarray(matrix, BF16)


def call(kernel, out_shape, flops=0, moved=0, **kwargs):
    return pl.pallas_call(
        kernel,
        out_shape=out_shape,
        compiler_params=pltpu.CompilerParams(vmem_limit_bytes=VMEM_LIMIT),
        cost_estimate=pl.CostEstimate(flops=flops, bytes_accessed=moved, transcendentals=0),
        **kwargs,
    )


def whole(shape):
    return pl.BlockSpec(shape, lambda *_: (0,) * len(shape))


def tiles_to_rows(get_tiles, swap, out_ref, groups):
    for group in range(groups):
        pair = jnp.concatenate([get_tiles(2 * group), get_tiles(2 * group + 1)], axis=1)
        turned = jnp.dot(swap, pair, preferred_element_type=F32).astype(BF16)
        for chunk in range(CHUNKS):
            cols = slice(chunk * LANES, (chunk + 1) * LANES)
            rows = turned[chunk * 16 : (chunk + 1) * 16]
            out_ref[group * 32 : group * 32 + 16, cols] = rows[:, :LANES]
            out_ref[group * 32 + 16 : group * 32 + 32, cols] = rows[:, LANES:]


def turn_rows(rows, swap):
    halves = [
        jnp.concatenate(
            [
                rows[side * 16 : side * 16 + 16, chunk * LANES : (chunk + 1) * LANES]
                for chunk in range(CHUNKS)
            ],
            axis=0,
        )
        for side in range(2)
    ]
    pair = jnp.concatenate(halves, axis=1)
    return jnp.dot(swap, pair, preferred_element_type=F32).astype(BF16)


def slots_kernel(caps, ids_ref, weight_ref, table_ref, scale_ref, slot_ref):
    top_k, tokens = ids_ref.shape
    experts = LANES
    lane = lax.broadcasted_iota(jnp.int32, (experts, tokens), 1)
    row = lax.broadcasted_iota(jnp.int32, (experts, tokens), 0)
    ids = ids_ref[...]
    weight = weight_ref[...].astype(F32)
    chosen = jnp.zeros((experts, tokens), F32)
    weights = jnp.zeros((experts, tokens), F32)
    for k in range(top_k):
        hit = ids[k : k + 1] == row
        chosen = jnp.where(hit, 1.0, chosen)
        weights = jnp.where(hit, weight[k : k + 1], weights)
    upper = jnp.where(row < lane, 1.0, 0.0).astype(BF16)
    counts = jnp.dot(chosen.astype(BF16), upper, preferred_element_type=F32)
    table = jnp.zeros((experts, LANES), F32)
    scales = jnp.zeros((experts, LANES), F32)
    from_end = (lane - tokens).astype(F32)
    for place in range(caps):
        mask = (chosen > 0.5) & (jnp.abs(counts - place) < 0.5)
        token = jnp.sum(jnp.where(mask, from_end, 0.0), axis=1, keepdims=True) + tokens
        scale = jnp.sum(jnp.where(mask, weights, 0.0), axis=1, keepdims=True)
        table = jnp.where(lane == place, token, table)
        scales = jnp.where(lane == place, scale, scales)
    table_ref[...] = table.T[:16].astype(jnp.int32)
    scale_ref[...] = scales.T[:16]
    slot_ref[...] = jnp.concatenate(
        [
            jnp.sum(jnp.where(ids[k : k + 1] == row, counts, 0.0), axis=0, keepdims=True)
            for k in range(top_k)
        ],
        axis=0,
    ).astype(jnp.int32)


def pack_rows_kernel(table_ref, hidden_ref, gain_ref, swap_ref, out_ref, normed):
    tokens, width = hidden_ref.shape
    step = pl.program_id(0)
    caps = out_ref.shape[0] // DESTS

    @pl.when(step == 0)
    def _():
        gain = gain_ref[...].astype(F32)
        gain = jnp.concatenate([gain[chunk : chunk + 1] for chunk in range(CHUNKS)], axis=1)
        swap = swap_ref[...]
        for start in range(0, tokens, 32):
            hidden = hidden_ref[start : start + 32].astype(F32)
            mean = jnp.sum(hidden * hidden, axis=1, keepdims=True) * (1.0 / width)
            low = (hidden * lax.rsqrt(mean + EPS) * gain).astype(BF16)
            turned = turn_rows(low, swap)
            for side in range(2):
                for inner in range(16):
                    normed[start + side * 16 + inner] = turned[
                        inner * 16 : (inner + 1) * 16, side * LANES : (side + 1) * LANES
                    ]
        normed[tokens] = jnp.zeros((CHUNKS, LANES), BF16)

    def fill(dest, carry):
        for place in range(caps):
            out_ref[dest * caps + place] = normed[table_ref[place, step * DESTS + dest]]
        return carry

    lax.fori_loop(0, DESTS, fill, 0, unroll=2)


def pack_grads_kernel(table_ref, scale_ref, grad_ref, out_ref):
    tokens = grad_ref.shape[0]
    step = pl.program_id(0)
    caps = out_ref.shape[0] // DESTS

    def fill(dest, carry):
        for place in range(caps):
            at = step * DESTS + dest
            token = jnp.minimum(table_ref[place, at], tokens - 1)
            scale = scale_ref[place, at]
            out_ref[dest * caps + place] = (grad_ref[token].astype(F32) * scale).astype(BF16)
        return carry

    lax.fori_loop(0, DESTS, fill, 0, unroll=2)


def expert_up_kernel(tile_ref, swap_ref, gate_w_ref, up_w_ref, row_ref, act_ref, da_ref, db_ref):
    rows = row_ref.shape[0]
    tiles_to_rows(
        lambda i: tile_ref[i * 256 : (i + 1) * 256], swap_ref[...], row_ref, rows // 32
    )
    gate = jnp.dot(row_ref[...], gate_w_ref[0], preferred_element_type=F32)
    up = jnp.dot(row_ref[...], up_w_ref[0], preferred_element_type=F32)
    sig = 1.0 / (1.0 + jnp.exp(-gate))
    silu = gate * sig
    act_ref[...] = (silu * up).astype(BF16)
    da_ref[...] = (up * sig * (1.0 + gate * (1.0 - sig))).astype(BF16)
    db_ref[...] = silu.astype(BF16)


def expert_down_kernel(
    caps,
    tile_ref,
    swap_ref,
    gather_ref,
    spread_ref,
    gate_w_ref,
    up_w_ref,
    down_w_ref,
    act_ref,
    da_ref,
    db_ref,
    grad_ref,
    pre_ref,
    upg_ref,
    back_ref,
    rowg,
):
    rows = grad_ref.shape[0]
    swap = swap_ref[...]
    tiles_to_rows(lambda i: tile_ref[i * 256 : (i + 1) * 256], swap, grad_ref, rows // 32)
    act_grad = lax.dot_general(grad_ref[...], down_w_ref[0], LAST, preferred_element_type=F32)
    pre = (act_grad * da_ref[...].astype(F32)).astype(BF16)
    upg = (act_grad * db_ref[...].astype(F32)).astype(BF16)
    pre_ref[...] = pre
    upg_ref[...] = upg
    score = jnp.sum(act_grad * act_ref[...].astype(F32), axis=1, keepdims=True)
    placed = jnp.dot(
        gather_ref[...],
        (score * spread_ref[...].astype(F32)).astype(BF16),
        preferred_element_type=F32,
    ).astype(BF16)
    rowg[...] = (
        lax.dot_general(pre, gate_w_ref[0], LAST, preferred_element_type=F32)
        + lax.dot_general(upg, up_w_ref[0], LAST, preferred_element_type=F32)
    ).astype(BF16)
    for group in range(rows // 32):
        halves = []
        for side in range(2):
            at = group * 32 + side * 16
            halves.append(
                jnp.concatenate(
                    [
                        rowg[at : at + 16, chunk * LANES : (chunk + 1) * LANES]
                        for chunk in range(CHUNKS)
                    ],
                    axis=0,
                )
            )
        turned = jnp.dot(
            swap, jnp.concatenate(halves, axis=1), preferred_element_type=F32
        ).astype(BF16)
        for side in range(2):
            for inner in range(16):
                row = group * 32 + side * 16 + inner
                place = (row % caps) * 16
                back_ref[row // caps, place : place + 16, :] = turned[
                    inner * 16 : (inner + 1) * 16, side * LANES : (side + 1) * LANES
                ]
    for source in range(rows // caps):
        back_ref[source, caps * 16 : caps * 16 + PACK_EXTRA, :] = jnp.broadcast_to(
            placed[source : source + 1], (PACK_EXTRA, LANES)
        )


def combine_kernel(
    ids_ref,
    slot_ref,
    back_hbm,
    hidden_ref,
    grad_ref,
    gain_ref,
    swap_ref,
    out_ref,
    score_ref,
    total,
    tiles,
    back_ref,
    load_sems,
):
    top_k, tokens = ids_ref.shape

    count = load_sems.shape[0]
    each = back_ref.shape[0] // count
    loads = [
        pltpu.make_async_copy(
            back_hbm.at[pl.ds(i * each, each)], back_ref.at[pl.ds(i * each, each)], load_sems.at[i]
        )
        for i in range(count)
    ]
    for load in loads:
        load.start()
    for load in loads:
        load.wait()

    def gather(token, carry):
        acc = jnp.zeros((CHUNKS, LANES), F32)
        for k in range(top_k):
            at = pl.multiple_of(slot_ref[k, token] * 16, 16)
            acc = acc + back_ref[ids_ref[k, token], pl.ds(at, 16), :].astype(F32)
        total[token] = acc
        return carry

    lax.fori_loop(0, tokens, gather, 0, unroll=4)
    gain = gain_ref[...].astype(F32)[None]
    share = 1.0 / (CHUNKS * LANES)

    def mean(value):
        return (
            jnp.sum(jnp.sum(value, axis=2, keepdims=True), axis=1, keepdims=True) * share
        )

    for start in range(0, tokens, 16):
        hidden = hidden_ref[start : start + 16].astype(F32)
        inv_rms = lax.rsqrt(mean(hidden * hidden) + EPS)
        unit = hidden * inv_rms
        scaled = total[start : start + 16] * gain
        residual = grad_ref[start : start + 16].astype(F32) + inv_rms * (
            scaled - unit * mean(scaled * unit)
        )
        tiles[start * 16 : start * 16 + 256] = residual.astype(BF16).reshape(256, LANES)
    tiles_to_rows(
        lambda i: tiles[i * 256 : (i + 1) * 256], swap_ref[...], out_ref, tokens // 32
    )
    extra = back_ref[:, back_ref.shape[1] - PACK_EXTRA :, :].astype(F32)
    score_ref[...] = (jnp.sum(extra, axis=1) * (1.0 / PACK_EXTRA)).astype(BF16)


def write_gate(ids, slot, weight, score, out_ref):
    top_k, tokens = ids.shape
    row = lax.broadcasted_iota(jnp.int32, (LANES, tokens), 0)
    found = []
    for k in range(top_k):
        hit = jnp.where(ids[k : k + 1] == row, 1.0, 0.0).astype(BF16)
        mine = lax.dot_general(score, hit, FIRST, preferred_element_type=F32)
        found.append(
            jnp.sum(jnp.where(slot[k : k + 1] == row, mine, 0.0), axis=0, keepdims=True)
        )
    scale = (CHUNKS * LANES) ** (-0.5)
    value = jnp.concatenate(found, axis=0) * scale / weight.astype(F32)
    out_ref[...] = value.astype(BF16)


def probs_kernel(query_ref, key_ref, begin_ref, out_ref):
    scores = lax.dot_general(
        query_ref[...], key_ref[...], LAST, preferred_element_type=F32
    ) * HEAD_DIM ** (-0.5)
    here = lax.broadcasted_iota(jnp.int32, (SEQ, SEQ), 0)
    there = lax.broadcasted_iota(jnp.int32, (SEQ, SEQ), 1)
    visible = (there <= here) & (there >= begin_ref[...])
    masked = jnp.where(visible, scores, -1e30)
    top = jnp.max(masked, axis=1, keepdims=True)
    weights = jnp.where(visible, jnp.exp(masked - top), 0.0)
    out_ref[0, 0] = (weights / jnp.sum(weights, axis=1, keepdims=True)).astype(BF16)


def tail_kernel(
    sum_scale,
    resid_hbm,
    weight_hbm,
    attn_hbm,
    probs_hbm,
    query_hbm,
    key_hbm,
    value_hbm,
    id_ref,
    slot_ref,
    pair_ref,
    score_ref,
    dq_ref,
    dk_ref,
    dv_ref,
    out_ref,
    gate_ref,
    group,
    weight,
    attn,
    probs,
    query,
    key,
    value,
    grads,
    acc,
    pieces,
    arrived,
    load_sems,
    ring_send,
    ring_recv,
    side_send,
    side_recv,
    dp_send,
    dp_recv,
):
    ep, dp = lax.axis_index("ep"), lax.axis_index("dp")
    chips = lax.axis_size("ep") // 2
    dp_size = lax.axis_size("dp")
    chip, core = ep // 2, ep % 2
    tokens, width = resid_hbm.shape
    half = tokens // 2
    above = ((chip + 1) % chips) * 2 + core
    below = ((chip + chips - 1) % chips) * 2 + core
    across = ((chip + 2) % chips) * 2 + core
    sibling = chip * 2 + 1 - core

    barrier = pltpu.get_barrier_semaphore()
    for peer in (above, below, sibling):
        pl.semaphore_signal(barrier, inc=1, device_id=(peer, dp), device_id_type=MESH)
    for step in range(1, dp_size):
        pl.semaphore_signal(
            barrier, inc=1, device_id=(ep, (dp + step) % dp_size), device_id_type=MESH
        )

    loads = [
        pltpu.make_async_copy(source, target, load_sems.at[number])
        for number, (source, target) in enumerate(
            (
                (resid_hbm, group.at[pl.ds(pl.multiple_of(ep * tokens, tokens), tokens)]),
                (weight_hbm, weight),
                (attn_hbm, attn),
                (query_hbm, query),
                (key_hbm, key),
                (value_hbm, value),
                (probs_hbm, probs),
            )
        )
    ]
    for load in loads:
        load.start()
    pl.semaphore_wait(barrier, dp_size - 1 + 3)

    def part(owner, second):
        at = pl.multiple_of(owner * tokens + second * half, half)
        return group.at[pl.ds(at, half)]

    def mine_at(second):
        return resid_hbm.at[pl.ds(second * half, half)]

    def ring(number, owner, second, target, source=None):
        return pltpu.make_async_remote_copy(
            src_ref=part(owner, second) if source is None else source,
            dst_ref=part(owner, second),
            send_sem=ring_send.at[number],
            recv_sem=ring_recv.at[number],
            device_id=(target, dp),
            device_id_type=MESH,
        )

    def side(number, owner, second, source=None):
        return pltpu.make_async_remote_copy(
            src_ref=part(owner, second) if source is None else source,
            dst_ref=part(owner, second),
            send_sem=side_send.at[number],
            recv_sem=side_recv.at[number],
            device_id=(sibling, dp),
            device_id_type=MESH,
        )

    first, second = mine_at(0), mine_at(1)
    up = [ring(0, ep, 0, above, first), ring(1, ep, 1, above, second)]
    down = [ring(3, ep, 0, below, first), ring(2, ep, 1, below, second)]
    own = [side(0, ep, 0, first), side(1, ep, 1, second)]
    for copy in (up[0], down[1], own[0], own[1], up[1], down[0]):
        copy.start()

    def matmuls(pair, last):
        at = pl.multiple_of(pair * 2 * tokens, 2 * tokens)
        mine = pl.ds(at, 2 * tokens)
        def add(step, carry):
            dest = (dp + 1 + step) % dp_size
            columns = pl.ds(pl.multiple_of(dest * tokens, tokens), tokens)
            product = lax.dot_general(
                group[mine, columns], attn[mine], FIRST, preferred_element_type=F32
            )
            if last is None:
                acc[dest] = product
            elif not last:
                acc[dest] = acc[dest] + product
            else:
                pieces[dest] = (acc[dest] + product).astype(BF16)
            return carry

        if not last:
            lax.fori_loop(0, dp_size, add, 0)
        else:
            for step in range(dp_size):
                add(step, 0)
                if step < dp_size - 1:
                    send_piece(step).start()
        grads[mine] = jnp.dot(group[mine], weight[...], preferred_element_type=F32).astype(BF16)

    def send_piece(step):
        dest = (dp + 1 + step) % dp_size
        return pltpu.make_async_remote_copy(
            src_ref=pieces.at[dest],
            dst_ref=arrived.at[dp],
            send_sem=dp_send.at[step],
            recv_sem=dp_recv.at[step],
            device_id=(ep, dest),
            device_id_type=MESH,
        )

    write_gate(id_ref[...], slot_ref[...], pair_ref[...], score_ref[...], gate_ref)
    loads[0].wait()
    own[0].wait_recv()
    own[1].wait_recv()
    loads[1].wait()
    loads[2].wait()
    matmuls(chip, None)

    up[0].wait_recv()
    forward_up = ring(4, below, 0, above)
    forward_up.start()
    relay = [side(2, below, 0)]
    relay[0].start()
    down[1].wait_recv()
    forward_down = ring(5, above, 1, below)
    forward_down.start()
    relay.append(side(3, above, 1))
    relay[1].start()
    up[1].wait_recv()
    relay.append(side(4, below, 1))
    relay[2].start()
    down[0].wait_recv()
    relay.append(side(5, above, 0))
    relay[3].start()
    for copy in relay:
        copy.wait_recv()
    matmuls(below // 2, False)
    matmuls(above // 2, False)
    forward_up.wait_recv()
    relay.append(side(6, across, 0))
    relay[4].start()
    forward_down.wait_recv()
    relay.append(side(7, across, 1))
    relay[5].start()
    relay[4].wait_recv()
    relay[5].wait_recv()
    matmuls(across // 2, True)

    for load in loads[3:]:
        load.wait()
    heads = query.shape[1] // HEAD_DIM
    scale = HEAD_DIM ** (-0.5)

    def attend(number, carry):
        seq, head = number // heads, number % heads
        at = (
            pl.ds(pl.multiple_of(seq * SEQ, SEQ), SEQ),
            pl.ds(pl.multiple_of(head * HEAD_DIM, HEAD_DIM), HEAD_DIM),
        )
        grad = grads[at]
        weights = probs[number]
        delta = jnp.sum(grad.astype(F32) * attn[at].astype(F32), axis=1, keepdims=True)
        prob_grad = lax.dot_general(grad, value[at], LAST, preferred_element_type=F32)
        score_grad = (weights.astype(F32) * (prob_grad - delta)).astype(BF16)
        dq_ref[at] = (
            jnp.dot(score_grad, key[at], preferred_element_type=F32) * scale
        ).astype(BF16)
        dk_ref[at] = (
            lax.dot_general(score_grad, query[at], FIRST, preferred_element_type=F32) * scale
        ).astype(BF16)
        dv_ref[at] = lax.dot_general(weights, grad, FIRST, preferred_element_type=F32).astype(BF16)
        return carry

    lax.fori_loop(0, probs.shape[0], attend, 0)

    for step in range(dp_size - 1):
        send_piece(step).wait_recv()
    total = pieces[dp].astype(F32)
    for step in range(1, dp_size):
        total = total + arrived[(dp + step) % dp_size].astype(F32)
    out_ref[...] = (total * sum_scale).astype(BF16)
    for copy in up + down + own + relay + [forward_up, forward_down]:
        copy.wait_send()
    for step in range(dp_size - 1):
        send_piece(step).wait_send()


def publish_kernel(*refs):
    count = len(refs) // 2
    for i in range(count):
        refs[count + i][...] = refs[i][...]


def publish(arrays):
    steps = 2
    blocks = [
        pl.BlockSpec((a.shape[0] // steps, a.shape[1]), lambda i: (i, 0))
        if a.shape[0] % (16 * steps) == 0
        else whole(a.shape)
        for a in arrays
    ]
    return call(
        publish_kernel,
        tuple(jax.ShapeDtypeStruct(a.shape, a.dtype) for a in arrays),
        moved=4000000,
        grid=(steps,),
        in_specs=blocks,
        out_specs=tuple(blocks),
    )(*arrays)


def per_device(
    hidden_state,
    out_grad,
    norm_gain,
    expert_ids,
    route_weight,
    w_gate,
    w_up,
    w_down,
    queries,
    keys,
    values,
    attn_out,
    out_weight,
    doc_start,
):
    tokens, width = hidden_state.shape
    top_k = expert_ids.shape[1]
    ff = w_gate.shape[2]
    dp_size = lax.axis_size("dp")
    experts = lax.axis_size("ep") * dp_size
    caps = 5 * tokens * top_k // (4 * experts)
    rows = experts * caps
    both = ("ep", "dp")
    swap = swap_matrix()
    hidden3 = hidden_state.reshape(tokens, CHUNKS, LANES)
    grad3 = out_grad.reshape(tokens, CHUNKS, LANES)
    gain2 = norm_gain.reshape(CHUNKS, LANES)

    ids_t, weight_t = expert_ids.T, route_weight.T
    table, scales, slots = call(
        functools.partial(slots_kernel, caps),
        (
            jax.ShapeDtypeStruct((16, experts), jnp.int32),
            jax.ShapeDtypeStruct((16, experts), F32),
            jax.ShapeDtypeStruct((top_k, tokens), jnp.int32),
        ),
        moved=300000,
    )(ids_t, weight_t)

    pack_block = pl.BlockSpec((DESTS * caps, CHUNKS, LANES), lambda i, *_: (i, 0, 0))

    def exchange(array):
        return lax.all_to_all(array, both, split_axis=0, concat_axis=0, tiled=True)

    def send(kernel, scalars, arrays, scratch):
        packed = call(
            kernel,
            jax.ShapeDtypeStruct((rows, CHUNKS, LANES), BF16),
            moved=6000000,
            grid_spec=pltpu.PrefetchScalarGridSpec(
                num_scalar_prefetch=len(scalars),
                grid=(experts // DESTS,),
                in_specs=[whole(a.shape) for a in arrays],
                out_specs=pack_block,
                scratch_shapes=scratch,
            ),
        )(*scalars, *arrays)
        return exchange(packed.reshape(experts, caps * 16, LANES)).reshape(rows * 16, LANES)

    table_scratch = [pltpu.VMEM((tokens + 1, CHUNKS, LANES), BF16)]
    got_rows = send(
        pack_rows_kernel, [table], [hidden_state, gain2, swap], table_scratch
    )
    got_grads = send(pack_grads_kernel, [table, scales], [grad3], [])

    group_len, head_cols = queries.shape
    head_count = head_cols // HEAD_DIM
    seq_count = group_len // SEQ
    head_block = pl.BlockSpec((SEQ, HEAD_DIM), lambda s, h: (s, h))
    probs_block = pl.BlockSpec((1, 1, SEQ, SEQ), lambda s, h: (s, h, 0, 0))
    probs = call(
        probs_kernel,
        jax.ShapeDtypeStruct((seq_count, head_count, SEQ, SEQ), BF16),
        flops=10**10,
        moved=5000000,
        grid=(seq_count, head_count),
        in_specs=[head_block, head_block, pl.BlockSpec((SEQ, 1), lambda s, h: (s, 0))],
        out_specs=probs_block,
    )(queries, keys, doc_start.reshape(group_len, 1))

    got_rows, probs, hidden3 = lax.optimization_barrier((got_rows, probs, hidden3))
    step_rows = SOURCES * caps
    steps = rows // step_rows
    flat_tiles = pl.BlockSpec((step_rows * 16, LANES), lambda i: (i, 0))
    wide = pl.BlockSpec((step_rows, width), lambda i: (i, 0))
    narrow = pl.BlockSpec((step_rows, ff), lambda i: (i, 0))
    w_in = whole((1, width, ff))
    w_out = whole((1, ff, width))
    narrow_shape = jax.ShapeDtypeStruct((rows, ff), BF16)
    wide_shape = jax.ShapeDtypeStruct((rows, width), BF16)
    rows_in, act, act_da, act_db = call(
        expert_up_kernel,
        (wide_shape, narrow_shape, narrow_shape, narrow_shape),
        flops=4 * rows * width * ff,
        moved=18000000,
        grid=(steps,),
        in_specs=[flat_tiles, whole((256, 256)), w_in, w_in],
        out_specs=(wide, narrow, narrow, narrow),
    )(got_rows, swap, w_gate, w_up)
    index = np.arange(step_rows)
    gather = jnp.asarray(index[None, :] // caps == np.arange(SOURCES)[:, None], BF16)
    spread = jnp.asarray(index[:, None] % caps == np.arange(LANES)[None, :], BF16)
    block_rows = caps * 16 + PACK_EXTRA
    scaled_grad, pre_grad, up_grad, send_back = call(
        functools.partial(expert_down_kernel, caps),
        (
            wide_shape,
            narrow_shape,
            narrow_shape,
            jax.ShapeDtypeStruct((experts, block_rows, LANES), BF16),
        ),
        flops=6 * rows * width * ff,
        moved=25000000,
        grid=(steps,),
        in_specs=[
            flat_tiles,
            whole((256, 256)),
            whole((SOURCES, step_rows)),
            whole((step_rows, LANES)),
            w_in,
            w_in,
            w_out,
            narrow,
            narrow,
            narrow,
        ],
        out_specs=(
            wide,
            narrow,
            narrow,
            pl.BlockSpec((SOURCES, block_rows, LANES), lambda i: (i, 0, 0)),
        ),
        scratch_shapes=[pltpu.VMEM((step_rows, width), BF16)],
    )(got_grads, swap, gather, spread, w_gate, w_up, w_down, act, act_da, act_db)
    back = exchange(send_back)
    grad_scale = (tokens * top_k) ** (-0.5)

    def weight_grad(left, right):
        product = lax.dot_general(left, right, FIRST, preferred_element_type=F32)
        return (product * grad_scale).astype(BF16)[None]

    grad_gate_w = weight_grad(rows_in, pre_grad)
    grad_up_w = weight_grad(rows_in, up_grad)
    grad_down_w = weight_grad(act, scaled_grad)

    back, grad_gate_w, grad_up_w, grad_down_w = lax.optimization_barrier(
        (back, grad_gate_w, grad_up_w, grad_down_w)
    )
    residual_grad, scores = call(
        combine_kernel,
        (
            jax.ShapeDtypeStruct((tokens, width), BF16),
            jax.ShapeDtypeStruct((experts, LANES), BF16),
        ),
        moved=8000000,
        grid_spec=pltpu.PrefetchScalarGridSpec(
            num_scalar_prefetch=2,
            grid=(1,),
            in_specs=[
                pl.BlockSpec(memory_space=pl.ANY),
                whole((tokens, CHUNKS, LANES)),
                whole((tokens, CHUNKS, LANES)),
                whole((CHUNKS, LANES)),
                whole((256, 256)),
            ],
            out_specs=(whole((tokens, width)), whole((experts, LANES))),
            scratch_shapes=[
                pltpu.VMEM((tokens, CHUNKS, LANES), F32),
                pltpu.VMEM((tokens * CHUNKS, LANES), BF16),
                pltpu.VMEM(back.shape, BF16),
                pltpu.SemaphoreType.DMA((8,)),
            ],
        ),
    )(ids_t, slots, back, hidden3, grad3, gain2, swap)
    any_spec = pl.BlockSpec(memory_space=pl.ANY)
    vmem_spec = pl.BlockSpec(memory_space=pltpu.VMEM)
    head_shape = jax.ShapeDtypeStruct((group_len, head_cols), BF16)
    head_vmem = pltpu.VMEM((group_len, head_cols), BF16)
    piece_shape = (dp_size, width // dp_size, head_cols)
    tail_results = pl.pallas_call(
        functools.partial(tail_kernel, (group_len * dp_size) ** (-0.5)),
        out_shape=(
            head_shape,
            head_shape,
            head_shape,
            jax.ShapeDtypeStruct(piece_shape[1:], BF16),
            jax.ShapeDtypeStruct((top_k, tokens), BF16),
        ),
        in_specs=[any_spec] * 7 + [vmem_spec] * 4,
        out_specs=(vmem_spec,) * 5,
        scratch_shapes=[
            pltpu.VMEM((group_len, width), BF16),
            pltpu.VMEM((width, head_cols), BF16),
            head_vmem,
            pltpu.VMEM((seq_count * head_count, SEQ, SEQ), BF16),
            head_vmem,
            head_vmem,
            head_vmem,
            head_vmem,
            pltpu.VMEM(piece_shape, F32),
            pltpu.VMEM(piece_shape, BF16),
            pltpu.VMEM(piece_shape, BF16),
            pltpu.SemaphoreType.DMA((7,)),
            pltpu.SemaphoreType.DMA((6,)),
            pltpu.SemaphoreType.DMA((6,)),
            pltpu.SemaphoreType.DMA((8,)),
            pltpu.SemaphoreType.DMA((8,)),
            pltpu.SemaphoreType.DMA((dp_size - 1,)),
            pltpu.SemaphoreType.DMA((dp_size - 1,)),
        ],
        compiler_params=pltpu.CompilerParams(
            collective_id=0, has_side_effects=True, vmem_limit_bytes=VMEM_LIMIT
        ),
        cost_estimate=pl.CostEstimate(
            flops=4 * 10**9, bytes_accessed=20000000, transcendentals=0
        ),
    )(
        residual_grad,
        out_weight,
        attn_out,
        probs.reshape(seq_count * head_count, SEQ, SEQ),
        queries,
        keys,
        values,
        ids_t,
        slots,
        weight_t,
        scores,
    )
    query_grad, key_grad, value_grad, out_weight_grad, gate_grad = publish(tail_results)
    return (
        gate_grad.T,
        grad_gate_w,
        grad_up_w,
        grad_down_w,
        residual_grad,
        out_weight_grad,
        query_grad,
        key_grad,
        value_grad,
    )


def solution(mesh):
    tokens = P(("dp", "ep"), None)
    expert = P(("ep", "dp"), None, None)
    heads = P("dp", "ep")
    return jax.shard_map(
        per_device,
        mesh=mesh,
        in_specs=(
            tokens,
            tokens,
            P(),
            tokens,
            tokens,
            expert,
            expert,
            expert,
            heads,
            heads,
            heads,
            heads,
            P(None, "ep"),
            P("dp"),
        ),
        out_specs=(tokens, expert, expert, expert, tokens, heads, heads, heads, heads),
        check_vma=False,
    )
```
